256 devices in a mesh: ctx: 32 (over x, z), exp: 8 (over y, core).
Axes of the slice: x: 4, y: 4, z: 8, core: 2. Of those that a mesh axis runs over, the one named last changes fastest.
Arguments:
- queries: bfloat16 [1, 128, 48, 128], P(None, None, 'exp'), may hold values from -8 to 8
- new_kv: bfloat16 [1, 128, 2, 8, 128], P(None, 'ctx', None, 'exp'), may hold values from -8 to 8
- kv_cache: bfloat16 [2, 8, 512, 128, 128], P(None, 'exp', 'ctx'), may hold values from -8 to 8
- residual: bfloat16 [1, 128, 6144], P(None, 'ctx', 'exp'), may hold values from -4 to 4
- kept_blocks: int32 [2, 8, 128, 4], P(None, 'exp'), may hold values from -1 to 511, as said below
- block_moves: int32 [1, 8, 512], P(None, 'exp'), may hold values from 0 to 511, as said below
- expert_ids: int32 [1, 128, 2], replicated, may hold values from 0 to 7, all different within a row; in each aligned block of 4 rows (0 to 3, 4 to 7, ..., all dimensions but the last counted through in order) at most 2 rows name the same one
- gate_weights: float32 [1, 128, 2], replicated, may hold values from 0.2 to 1
- norm_gain: float32 [6144], replicated, may hold values from 0.1 to 1.9
- expert_in: bfloat16 [8, 2, 6144, 8192], P('exp', None, None, 'ctx'), may hold values from -0.078125 to 0.078125
- expert_out: bfloat16 [8, 8192, 6144], P('exp', 'ctx'), may hold values from -0.0625 to 0.0625
Outputs:
- layer_out: bfloat16 [1, 128, 6144], P(None, 'ctx', 'exp')
- final_cache: bfloat16 [2, 8, 512, 128, 128], P(None, 'exp', 'ctx')
The draws below stay inside these ranges and needn't reach their ends.
Inputs may be any that keep to these rules, and one draw needn't show every extreme that they name: kept_blocks[s, h, b] lists slots of head h holding blocks of sequence b that step s attends; -1 marks an empty entry. A slot is listed at most once for a step and head. For each step and head, block_moves is a permutation of the 512 slots. The slots held by one index of ctx go to at most 1 slots of any one index of ctx, and to exactly 1 of some. `expert_ids`: each row names two different experts. Among the 4 tokens of one index of ctx (aligned blocks of 4 rows) no expert is named by more than 2 rows, and one is named by exactly 2.
All inputs are finite; a program needn't handle non-finite values.
Results may differ from the reference program's by a relative error of at most 0.013.
Values may be sent and summed in bfloat16 or wider, within the bound.
A program may use at most 128 MiB of HBM per device.

```python
import math
import jax
import jax.numpy as jnp
import numpy as np
from jax import lax

D = 6144
QH = 48
KEY_VALUE_HEADS = 8
HEAD_SIZE = 128
NEXP = 8
FF = 8192
BLOCK_ROWS = 128
STEPS = 1
TB = 4
RETAINED_BLOCKS = 4
BATCH_SEQUENCES = 128
CONTEXT_SLOTS = 16
HEAD_SLOTS = 512
CAPM = 1
CAPE = 2
N_CTX = 32


def block_layout(key):
    key_per_head = jax.random.split(jax.random.fold_in(key, 11), KEY_VALUE_HEADS)
    put_down = jax.vmap(lambda lone_item: jax.random.permutation(lone_item, HEAD_SLOTS))(key_per_head).astype(jnp.int32).reshape(KEY_VALUE_HEADS, BATCH_SEQUENCES, RETAINED_BLOCKS)
    lifetime = jax.random.randint(jax.random.fold_in(key, 12), (KEY_VALUE_HEADS, BATCH_SEQUENCES, RETAINED_BLOCKS), 1, STEPS + 2)
    lifetime = lifetime.at[:, :, 0].set(STEPS + 1)
    group_count = CONTEXT_SLOTS // CAPM
    devices = jnp.arange(N_CTX, dtype=jnp.int32)[None, :, None]
    head_index = jnp.arange(KEY_VALUE_HEADS, dtype=jnp.int32)[:, None, None]
    lists = []
    moves = []
    for step in range(STEPS + 1):
        lists.append(jnp.where(lifetime > step, put_down, -1).astype(jnp.int32))
        if step < STEPS:
            step_key = jax.random.fold_in(key, 20 + step)
            offset_keys = jax.random.split(jax.random.fold_in(step_key, 1), KEY_VALUE_HEADS)
            offsets = jax.vmap(lambda lone_item: jax.random.permutation(lone_item, N_CTX)[:group_count])(offset_keys).astype(jnp.int32)
            order_keys = jax.random.split(jax.random.fold_in(step_key, 2), KEY_VALUE_HEADS * N_CTX)
            orders = jax.vmap(lambda lone_item: jax.random.permutation(lone_item, CONTEXT_SLOTS))(order_keys).astype(jnp.int32).reshape(KEY_VALUE_HEADS, N_CTX, CONTEXT_SLOTS)
            shuffle_keys = jax.random.split(jax.random.fold_in(step_key, 3), KEY_VALUE_HEADS * N_CTX)
            shuffles = jax.vmap(lambda lone_item: jax.random.permutation(lone_item, CONTEXT_SLOTS))(shuffle_keys).astype(jnp.int32).reshape(KEY_VALUE_HEADS, N_CTX, CONTEXT_SLOTS)
            group = orders // CAPM
            within = orders % CAPM
            aimed_place = (devices + offsets[head_index, group]) % N_CTX
            location = shuffles[head_index, aimed_place, group * CAPM + within]
            target_place = (aimed_place * CONTEXT_SLOTS + location).reshape(KEY_VALUE_HEADS, HEAD_SLOTS).astype(jnp.int32)
            moves.append(target_place)
            put_down = target_place[head_index, put_down]
    return (jnp.stack(lists), jnp.stack(moves))


def draw_kept_blocks(key, part):
    lists, moves = block_layout(key)
    return lists


def draw_block_moves(key, part):
    lists, moves = block_layout(key)
    return moves


def draw_queries(key, part):
    key = jax.random.fold_in(key, 3)
    form_dims = (STEPS, BATCH_SEQUENCES, QH, HEAD_SIZE)
    values = jax.random.truncated_normal(key, -6.0, 6.0, form_dims, jnp.float32)
    return values.astype(jnp.bfloat16)


def draw_new_kv(key, part):
    key = jax.random.fold_in(key, 4)
    form_dims = (STEPS, BATCH_SEQUENCES, 2, KEY_VALUE_HEADS, HEAD_SIZE)
    values = jax.random.truncated_normal(key, -6.0, 6.0, form_dims, jnp.float32)
    return values.astype(jnp.bfloat16)


def draw_kv_cache(key, part):
    key = jax.random.fold_in(key, 5)
    form_dims = (2, KEY_VALUE_HEADS, HEAD_SLOTS, BLOCK_ROWS, HEAD_SIZE)
    values = jax.random.truncated_normal(key, -6.0, 6.0, form_dims, jnp.float32)
    return values.astype(jnp.bfloat16)


def levels(key, dims, pieces, low, largest):
    gain = 1.0
    for axis_at, blocks in pieces:
        heights = jax.random.uniform(jax.random.fold_in(jax.random.fold_in(key, 6), axis_at), (blocks,), jnp.float32, low / len(pieces), largest / len(pieces))
        gain = gain * jnp.repeat(jnp.exp(heights), dims[axis_at] // blocks).reshape((-1,) + (1,) * (len(dims) - 1 - axis_at))
    return gain


def assign_block(stream_key, own, number, rows, count, top, bound, skew):
    ranking = jax.random.permutation(stream_key, count)
    heavy_load, ordinary = load_shares(count, rows * top, bound, skew, True), load_shares(count, rows * top, bound, skew, False)
    places = jnp.arange(count)

    def named(lengths, turn):
        used = int((lengths > 0).sum())
        fixed = max(1, used // 4)
        passed = fixed + (places - fixed + turn * (used - fixed)) % max(1, count - fixed)
        return jnp.zeros((count,), jnp.int32).at[ranking[jnp.where(places < fixed, places, passed)]].set(jnp.asarray(lengths, jnp.int32))

    lengths = jnp.where(number % 4 == 0, named(heavy_load, number // 4), named(ordinary, number - number // 4 - 1))
    mixed = jax.random.permutation(jax.random.fold_in(own, 3), count)
    source_of, taker = mixed[0:count // 2 * 2:2], mixed[1:count // 2 * 2:2]
    room = jnp.minimum(lengths[source_of] - 1, bound - lengths[taker]) // 2
    room = jnp.where((source_of == ranking[0]) | (taker == ranking[0]) | (lengths[taker] == 0), 0, jnp.maximum(room, 0))
    passed = jax.random.randint(jax.random.fold_in(own, 4), (count // 2,), 0, 1 << 20) % (room + 1)
    lengths = lengths.at[source_of].add(-passed).at[taker].add(passed)
    labels = jnp.searchsorted(jnp.cumsum(lengths), jnp.arange(rows * top), side="right").astype(jnp.int32)
    listing = labels.reshape(top, rows).T
    listing = listing[jax.random.permutation(jax.random.fold_in(own, 1), rows)]
    turn = jax.random.randint(jax.random.fold_in(own, 2), (rows, 1), 0, top)
    return jnp.take_along_axis(listing, (jnp.arange(top)[None, :] + turn) % top, axis=1)


def load_shares(number_of, total, limit, lean, full):
    portions = [(1 << 20) // math.isqrt(rank ** lean) + 1 for rank in range(1, number_of + 1)]
    largest = limit if full else min(limit, max(-(-total // number_of), total * portions[0] // sum(portions)))
    least = 1 if total - largest >= number_of - 1 else 0
    given, rest = [largest] + [least] * (number_of - 1), total - largest - least * (number_of - 1)
    while rest > 0:
        candidates = [i for i in range(1, number_of) if given[i] < largest] or [i for i in range(1, number_of) if given[i] < limit]
        whole, budget = sum([portions[i] for i in candidates]), rest
        for i in candidates:
            more = min(limit - given[i], max(1, budget * portions[i] // whole), rest)
            given[i] = given[i] + more
            rest = rest - more
    return np.array(given)


def bell_draw(rng, dims, scale, bound, cuts=(), held_as=jnp.bfloat16):
    level = levels(rng, dims, cuts, -0.22, 0.18) if cuts else 1.0
    result = jax.random.normal(rng, dims, jnp.float32) * scale * level
    return jnp.minimum(jnp.maximum(result, -bound), bound).astype(held_as)


def setup_inputs(seed: int = 0) -> dict:
    splits = jax.random.split(jax.random.key(seed), 12)
    queries = draw_queries(jax.random.fold_in(splits[11], 71), 0)
    new_kv = draw_new_kv(jax.random.fold_in(splits[11], 71), 0)
    kv_cache = draw_kv_cache(jax.random.fold_in(splits[11], 71), 0)
    residual = bell_draw(splits[3], (STEPS, BATCH_SEQUENCES, D), 0.25, 4.0, ((1, 32), (2, 8)))
    kept_blocks = draw_kept_blocks(jax.random.fold_in(splits[11], 71), 0)
    block_moves = draw_block_moves(jax.random.fold_in(splits[11], 71), 0)
    expert_ids_keys = jax.random.split(jax.random.fold_in(splits[6], 1), STEPS * BATCH_SEQUENCES // TB)
    expert_ids_turns = jax.random.permutation(jax.random.fold_in(splits[6], 3), STEPS * BATCH_SEQUENCES // TB)
    expert_ids = jax.vmap(lambda own, number: assign_block(jax.random.fold_in(splits[6], 2), own, number, TB, NEXP, 2, CAPE, 2))(expert_ids_keys, expert_ids_turns).reshape((STEPS, BATCH_SEQUENCES, 2))
    gate_weights = jnp.clip(jax.random.uniform(splits[7], (STEPS, BATCH_SEQUENCES, 2), jnp.float32, 0.2, 1.0), 0.2, 1.0)
    norm_gain = jnp.clip(1.0 + 0.18 * jax.random.normal(splits[8], (D,), jnp.float32), 0.1, 1.9)
    expert_in = bell_draw(splits[9], (NEXP, 2, D, FF), D ** -0.5, 0.078125, ((0, 8), (3, 32)))
    expert_out = bell_draw(splits[10], (NEXP, FF, D), FF ** -0.5, 0.0625, ((0, 8), (1, 32)))
    return dict(queries=queries, new_kv=new_kv, kv_cache=kv_cache, residual=residual, kept_blocks=kept_blocks, block_moves=block_moves, expert_ids=expert_ids, gate_weights=gate_weights, norm_gain=norm_gain, expert_in=expert_in, expert_out=expert_out)


NEG = -1e+30
EPS = 1e-05

def reference(queries, new_kv, kv_cache, residual, kept_blocks, block_moves, expert_ids, gate_weights, norm_gain, expert_in, expert_out):
    scale = 1.0 / math.sqrt(HEAD_SIZE)
    per_group = QH // KEY_VALUE_HEADS
    head_list = jnp.arange(KEY_VALUE_HEADS, dtype=jnp.int32)[:, None, None]
    cache = kv_cache
    outputs = []
    for step in range(STEPS):
        listed = kept_blocks[step]
        valid = listed >= 0
        safe_ids = jnp.where(valid, listed, 0).astype(jnp.int32)
        keys_wide = cache[0][head_list, safe_ids].astype(jnp.float32)
        values_wide = cache[1][head_list, safe_ids].astype(jnp.float32)
        queried = queries[step].reshape(BATCH_SEQUENCES, KEY_VALUE_HEADS, per_group, HEAD_SIZE).astype(jnp.float32)
        scores = jnp.einsum('bhqd,hbord->hbqor', queried, keys_wide, precision=lax.Precision.HIGHEST) * scale
        block_max = lax.optimization_barrier(jnp.max(scores, axis=-1))
        probs = lax.optimization_barrier(jnp.exp(scores - block_max[..., None]).astype(jnp.bfloat16))
        probs = probs.astype(jnp.float32)
        block_sum = lax.optimization_barrier(jnp.sum(probs, axis=-1))
        block_out = jnp.einsum('hbqor,hbord->hbqod', probs, values_wide, precision=lax.Precision.HIGHEST)
        valid_wide = valid[:, :, None, :]
        block_max = jnp.where(valid_wide, block_max, NEG)
        block_sum = jnp.where(valid_wide, block_sum, 0.0)
        block_out = jnp.where(valid_wide[..., None], block_out, 0.0)
        own_key = new_kv[step, :, 0].astype(jnp.float32)
        own_value = new_kv[step, :, 1].astype(jnp.float32)
        own_score = jnp.einsum('bhqd,bhd->hbq', queried, own_key, precision=lax.Precision.HIGHEST) * scale
        highest = jnp.maximum(lax.optimization_barrier(jnp.max(block_max, axis=-1)), own_score)
        factor = jnp.exp(block_max - highest[..., None])
        fresh = jnp.exp(own_score - highest)
        total = lax.optimization_barrier(jnp.sum(factor * block_sum, axis=-1)) + fresh
        summed = jnp.einsum('hbqo,hbqod->hbqd', factor, block_out, precision=lax.Precision.HIGHEST)
        summed = summed + fresh[..., None] * jnp.transpose(own_value, (1, 0, 2))[:, :, None, :]
        attention = jnp.transpose(summed / total[..., None], (1, 0, 2, 3)).reshape(BATCH_SEQUENCES, D)
        hidden_in = (residual[step].astype(jnp.float32) + attention).astype(jnp.bfloat16)
        wide = hidden_in.astype(jnp.float32)
        normed = (wide * lax.rsqrt(lax.optimization_barrier(jnp.mean(wide * wide, axis=-1, keepdims=True)) + EPS) * norm_gain).astype(jnp.bfloat16)

        def expert_apply(index):
            gate_part = jnp.dot(normed, expert_in[index, 0], preferred_element_type=jnp.float32)
            upper_part = jnp.dot(normed, expert_in[index, 1], preferred_element_type=jnp.float32)
            activated = (jax.nn.silu(gate_part) * upper_part).astype(jnp.bfloat16)
            return jnp.dot(activated, expert_out[index], preferred_element_type=jnp.float32)
        produced = lax.map(expert_apply, jnp.arange(NEXP, dtype=jnp.int32))
        picked = produced[expert_ids[step], jnp.arange(BATCH_SEQUENCES, dtype=jnp.int32)[:, None]]
        mixed = lax.optimization_barrier(jnp.sum(gate_weights[step][..., None] * picked, axis=1))
        outputs.append((wide + mixed).astype(jnp.bfloat16))
        moved = jnp.zeros_like(cache).at[:, jnp.arange(KEY_VALUE_HEADS, dtype=jnp.int32)[:, None], block_moves[step]].set(cache)
        successor = kept_blocks[step + 1]
        successor_index = jnp.where(successor >= 0, successor, 0).astype(jnp.int32)
        still_living = jnp.zeros((KEY_VALUE_HEADS, HEAD_SLOTS), jnp.int32).at[head_list, successor_index].max((successor >= 0).astype(jnp.int32))
        cache = jnp.where(still_living[None, :, :, None, None] > 0, moved, jnp.zeros_like(moved))
    return (jnp.stack(outputs), cache)
```

```python
import functools
import math

import jax
import jax.numpy as jnp
from jax import lax
from jax.experimental import pallas as pl
from jax.experimental.pallas import tpu as pltpu
from jax.sharding import PartitionSpec as P

MESH = pl.DeviceIdType.MESH
NEG = -1e30
EPS = 1e-05
F32, BF16, I32 = jnp.float32, jnp.bfloat16, jnp.int32

DZ_ORDER = (4, 3, 5, 2, 6, 1, 7, 0)
ORDER = tuple((dx, dz) for dz in DZ_ORDER for dx in (2, 1, 3, 0) if (dx, dz) != (0, 0))
PACE = (0, 4, 4, 4, 8, 8, 3, 0)


def iota(shape, dim):
    return lax.broadcasted_iota(I32, shape, dim)


def dot(a, b):
    return jnp.dot(a, b, preferred_element_type=F32)


def dot_nt(a, b):
    return lax.dot_general(a, b, (((1,), (1,)), ((), ())), preferred_element_type=F32)


def split3(v):
    first = v.astype(BF16).astype(F32)
    second = (v - first).astype(BF16).astype(F32)
    return first, second, v - first - second


def kernel(
    moves_hbm, kept_hbm, cache_hbm, q_hbm, nkv_hbm, res_hbm, ids_hbm, gates_hbm, gain_hbm, win_hbm, wout_hbm,
    lay_ref, fin_ref,
    moves_ref, kept_ref, cache, q_ref, nkv_ref, res_ref, ids_ref, gates_ref, gain_ref, win, wout, idxv, idxs, send_a, recv_a, gx, send_e, recv_e, send_f, recv_f, send_g, recv_g, send_h, recv_h,
    send_r, recv_r, scr, nks, nvs, slots, gatev, selt, att_s, res_s,
    lsem, sa, ra, sc, rc, sd, rd, se, re, sf, rf, sg, rg, sh, rh, sr, rr,
):
    c = lax.axis_index("ctx")
    e = lax.axis_index("exp")
    x, z = lax.div(c, 8), lax.rem(c, 8)
    y, k = lax.div(e, 2), lax.rem(e, 2)
    scale = 1.0 / math.sqrt(128)

    def ctx_at(dx, dz):
        return lax.rem(x + dx, 4) * 8 + lax.rem(z + dz, 8)

    def exp_at(dy, dk):
        return lax.rem(y + dy, 4) * 2 + lax.rem(k + dk, 2)

    def remote(src, dst, s, r, ctx=None, exp=None):
        return pltpu.make_async_remote_copy(
            src_ref=src, dst_ref=dst, send_sem=s, recv_sem=r,
            device_id=(c if ctx is None else ctx, e if exp is None else exp), device_id_type=MESH,
        )

    sources = (moves_hbm, kept_hbm, cache_hbm, q_hbm, nkv_hbm, res_hbm, ids_hbm, gates_hbm, gain_hbm, win_hbm, wout_hbm)
    targets = (moves_ref, kept_ref, cache, q_ref, nkv_ref, res_ref, ids_ref, gates_ref, gain_ref, win, wout)
    loads = [pltpu.make_async_copy(a, b, lsem.at[i]) for i, (a, b) in enumerate(zip(sources, targets))]
    for load in loads[:9]:
        load.start()

    barrier = pltpu.get_barrier_semaphore()

    def greet_ctx(o, carry):
        pl.semaphore_signal(
            barrier, inc=1, device_id=(ctx_at(lax.div(o, 8), lax.rem(o, 8)), e), device_id_type=MESH
        )
        return carry

    def greet_exp(o, carry):
        pl.semaphore_signal(
            barrier, inc=1, device_id=(c, exp_at(lax.div(o, 2), lax.rem(o, 2))), device_id_type=MESH
        )
        return carry

    lax.fori_loop(1, 32, greet_ctx, 0)
    lax.fori_loop(1, 8, greet_exp, 0)

    loads[0].wait()
    loads[1].wait()
    mv = moves_ref[...]
    lane = iota((32, 512), 1)
    off = iota((32, 512), 0)
    target = ((x + (off >> 3)) & 3) * 8 + ((z + (off & 7)) & 7)
    hit = ((mv >> 4) == target) & ((lane >> 4) == c)
    srcj = jnp.max(jnp.where(hit, lane & 15, 0), axis=1, keepdims=True)
    lane = iota((16, 512), 1)
    hit = mv == 16 * c + iota((16, 512), 0)
    place = ((x - (lane >> 7)) & 3) * 8 + ((z - ((lane >> 4) & 7)) & 7)
    rslot = jnp.max(jnp.where(hit, place, 0), axis=1, keepdims=True)
    kept1 = kept_ref[1]
    slot16 = 16 * c + iota((16, 128), 0)
    alive = kept1[0:1] == slot16
    for j in range(1, 4):
        alive = alive | (kept1[j : j + 1] == slot16)
    living = jnp.max(jnp.where(alive, 1, 0), axis=1, keepdims=True)
    eye32 = iota((32, 128), 0) == iota((32, 128), 1)
    eye16 = iota((16, 128), 0) == iota((16, 128), 1)
    idxv[0:1, :] = jnp.sum(jnp.where(eye32, srcj, 0), axis=0, keepdims=True)
    idxv[1:2, :] = jnp.sum(jnp.where(eye16, rslot, 0), axis=0, keepdims=True)
    idxv[2:3, :] = jnp.sum(jnp.where(eye16, living, 0), axis=0, keepdims=True)
    to_smem = pltpu.make_async_copy(idxv, idxs, lsem.at[11])
    to_smem.start()

    loads[2].wait()
    loads[9].start()
    loads[10].start()
    to_smem.wait()

    def pack(o, carry):
        send_r[o] = cache[:, idxs[0, o]]
        return carry

    lax.fori_loop(0, 32, pack, 0)

    pl.semaphore_wait(barrier, 38)

    def copy_a(o):
        dx, dz = lax.div(o, 8), lax.rem(o, 8)
        t = ctx_at(dx, dz)
        return remote(send_a.at[t], recv_a.at[o], sa.at[o], ra.at[o], ctx=t)

    def copy_r(o, dx, dz):
        return remote(send_r.at[o], recv_r.at[o], sr.at[o], rr.at[o], ctx=ctx_at(dx, dz))

    done = [0]

    def relocate(count):
        for dx, dz in ORDER[done[0] : done[0] + count]:
            copy_r(dx * 8 + dz, dx, dz).start()
        done[0] += count

    def loop(lo, hi, body):
        def step(o, carry):
            body(o)
            return carry

        lax.fori_loop(lo, hi, step, 0)

    relocate(PACE[0])

    rsub, rlane = iota((128, 128), 0), iota((128, 128), 1)
    kept0 = kept_ref[0]
    slot_id = 16 * c + (rsub & 15)
    owned = kept0[0:1] == slot_id
    for j in range(1, 4):
        owned = owned | (kept0[j : j + 1] == slot_id)
    owned = owned & (rsub < 96)
    ownf = jnp.where(owned, 1.0, 0.0)
    ownb = ownf.astype(BF16)
    owncol = jnp.sum(jnp.where(owned, rlane, 0), axis=1, keepdims=True)
    ownrow = dot_nt(iota((8, 128), 1).astype(F32).astype(BF16), ownb)[0:1].astype(I32)
    loads[3].wait()
    heads = [dot(ownb[16 * i : 16 * i + 16], q_ref[i]) for i in range(6)]
    q96 = jnp.concatenate(heads + [jnp.zeros((32, 128), F32)], axis=0).astype(BF16)
    scores = jnp.zeros((128, 128), F32)
    for j in range(16):
        scores = jnp.where((rsub & 15) == j, dot_nt(q96, cache[0, j]), scores)
    scores = scores * scale
    m = jnp.max(scores, axis=1, keepdims=True)
    probs = jnp.exp(scores - m).astype(BF16)
    l = jnp.sum(probs.astype(F32), axis=1, keepdims=True)
    out = jnp.zeros((128, 128), F32)
    for j in range(16):
        out = jnp.where((rsub & 15) == j, dot(probs, cache[1, j]), out)
    eye = rsub == rlane
    same = (owncol == ownrow) & ((rsub >> 4) == (rlane >> 4))
    mrow = jnp.sum(jnp.where(eye, m, 0.0), axis=0, keepdims=True)
    mseq = jnp.max(jnp.where(same, mrow, NEG), axis=1, keepdims=True)
    f = jnp.exp(m - mseq)
    lrow = jnp.sum(jnp.where(eye, l * f, 0.0), axis=0, keepdims=True)
    lseq = jnp.sum(jnp.where(same, lrow, 0.0), axis=1, keepdims=True)
    first = jnp.min(jnp.where(same, rlane.astype(F32), 999.0), axis=1, keepdims=True)
    place = ((rsub >> 4) << 2) + (owncol & 3)
    spread = (place == rlane) & (first == rsub.astype(F32)) & (rsub < 96)
    stats = [jnp.where(spread, v, 0.0).astype(BF16) for v in split3(mseq) + split3(lseq)]
    rl = iota((1, 128), 1)
    code = jnp.where(rl < 96, ((ownrow >> 2) << 5) + ((rl >> 4) << 2) + (ownrow & 3), -1)
    lift = jnp.where(iota((1024, 128), 0) == code, 1.0, 0.0).astype(BF16)
    values = dot(lift, (out * f).astype(BF16)).reshape(32, 32, 128)
    code = jnp.where(rl < 96, (ownrow >> 2) << 3, -100)
    row256 = iota((256, 128), 0)
    lift = jnp.concatenate([jnp.where(row256 == code + t, 1.0, 0.0).astype(BF16) for t in range(6)], axis=1)
    stat = dot(lift, jnp.concatenate(stats, axis=0)).reshape(32, 8, 128)
    send_a[...] = jnp.concatenate([values[:, 0:24], stat], axis=1).astype(BF16)

    loop(1, 32, lambda o: copy_a(o).start())
    relocate(PACE[1])
    recv_a[0] = send_a[c]

    for load in loads[4:9]:
        load.wait()
    res = res_ref[...].astype(F32)
    nks[0:4] = nkv_ref[:, 0].astype(F32)
    nks[4:8] = nkv_ref[:, 0].astype(F32)
    nvs[0:4] = nkv_ref[:, 1].astype(F32)
    nvs[4:8] = nkv_ref[:, 1].astype(F32)
    for i in range(6):
        res_s[4 * i : 4 * i + 4] = res[:, 128 * i : 128 * i + 128]
    s8, b8 = iota((8, 128), 0), iota((8, 128), 1)
    low = jnp.where((s8 < 4) & (b8 == 4 * c + s8), 1.0, 0.0).astype(BF16)
    high = jnp.where((s8 >= 4) & (b8 == 4 * c + s8 - 4), 1.0, 0.0).astype(BF16)
    q24 = jnp.concatenate([dot(low, q_ref[2 * p]) + dot(high, q_ref[2 * p + 1]) for p in range(3)], axis=0)
    nk24 = jnp.concatenate([nks[...]] * 3, axis=0)
    nv24 = jnp.concatenate([nvs[...]] * 3, axis=0)
    own_score = jnp.sum(q24 * nk24, axis=1, keepdims=True) * scale
    eye24 = iota((24, 128), 0) == iota((24, 128), 1)
    own_score = jnp.sum(jnp.where(eye24, own_score, 0.0), axis=0, keepdims=True)

    g3 = split3(gates_ref[...])
    scr[0:2] = ids_ref[...].astype(F32)
    for i in range(3):
        scr[2 * i + 2 : 2 * i + 4] = g3[i]
    o128 = rlane >> 2
    group = ((x - (o128 >> 3)) & 3) * 8 + ((z - (o128 & 7)) & 7)
    relative = jnp.where(rsub == 4 * group + (rlane & 3), 1.0, 0.0).astype(BF16)
    routed = dot(scr[...].astype(BF16), relative)
    r0, r1 = routed[0:1].astype(I32), routed[1:2].astype(I32)
    w0 = routed[2:3] + routed[4:5] + routed[6:7]
    w1 = routed[3:4] + routed[5:6] + routed[7:8]
    goes = jnp.where((r0 == s8) | (r1 == s8), 1, 0)
    rank = jnp.zeros((8, 128), I32)
    for d in range(1, 4):
        rank = rank + jnp.where((b8 & 3) >= d, pltpu.roll(goes, d, 1), 0)
    slot = jnp.where(goes > 0, ((b8 >> 2) << 1) + rank, -1)
    slots[...] = slot
    gatev[...] = jnp.where(r0 == s8, w0, 0.0) + jnp.where(r1 == s8, w1, 0.0)
    row64 = iota((64, 128), 0)
    sel = jnp.concatenate([jnp.where(row64 == slot[j : j + 1], 1.0, 0.0) for j in range(8)], axis=0)
    selt[...] = sel.T.astype(BF16)
    sel = sel.astype(BF16)
    gate_col = jnp.sum(
        jnp.where(row64 == slots[pl.ds(e, 1)], gatev[pl.ds(e, 1)], 0.0), axis=1, keepdims=True
    )

    loop(1, 32, lambda o: copy_a(o).wait_recv())
    got = recv_a[...].astype(F32)
    st = got[:, 24:32]
    qi = iota((32, 8, 128), 1)
    m = jnp.sum(jnp.where(qi < 3, st, 0.0), axis=1, keepdims=True)
    l = jnp.sum(jnp.where((qi >= 3) & (qi < 6), st, 0.0), axis=1, keepdims=True)
    m = jnp.where(l > 0, m, NEG)
    top = jnp.maximum(jnp.max(m, axis=0), own_score)
    w = jnp.where(l > 0, jnp.exp(m - top[None]), 0.0)
    fresh = jnp.exp(own_score - top)
    inv_den = 1.0 / (jnp.sum(w * l, axis=0) + fresh)
    w = w * inv_den[None]
    wcol = jnp.sum(jnp.where(eye24[None], jnp.broadcast_to(w, (32, 24, 128)), 0.0), axis=2, keepdims=True)
    att = jnp.sum(wcol * got[:, 0:24], axis=0)
    fcol = jnp.sum(jnp.where(eye24, fresh * inv_den, 0.0), axis=1, keepdims=True)
    att = att + fcol * nv24
    hidden = (res_s[...] + att).astype(BF16).astype(F32)
    gx[0, 0] = jnp.concatenate([hidden, jnp.zeros((8, 128), F32)], axis=0).astype(BF16)

    def copy_c(dz):
        return remote(gx.at[0, 0], gx.at[0, dz], sc.at[dz], rc.at[dz], ctx=ctx_at(0, dz))

    def copy_d(dx):
        return remote(gx.at[0], gx.at[dx], sd.at[dx], rd.at[dx], ctx=ctx_at(dx, 0))

    loop(1, 8, lambda dz: copy_c(dz).start())
    relocate(PACE[2])
    loop(1, 8, lambda dz: copy_c(dz).wait_recv())
    loop(1, 4, lambda dx: copy_d(dx).start())
    relocate(PACE[3])
    loop(1, 4, lambda dx: copy_d(dx).wait_recv())

    flat = gx[...].reshape(32, 32, 128).astype(F32).reshape(16, 2, 32, 128)
    sub16 = iota((16, 8, 128), 1)
    parts = []
    for p in range(3):
        one, two = flat[:, 0, 8 * p : 8 * p + 8], flat[:, 1, 8 * p : 8 * p + 8]
        parts.append(jnp.where(sub16 < 4, one, pltpu.roll(two, 4, 1)).reshape(128, 128).astype(BF16))
        parts.append(jnp.where(sub16 < 4, pltpu.roll(one, 4, 1), two).reshape(128, 128).astype(BF16))
    tokens = jnp.concatenate(parts, axis=1)

    def copy_e(o):
        t = exp_at(lax.div(o, 2), lax.rem(o, 2))
        return remote(send_e.at[t], recv_e.at[e], se.at[o], re.at[o], exp=t)

    for j in range(8):
        send_e[j] = dot(sel[64 * j : 64 * j + 64], tokens).astype(BF16)
    loop(1, 8, lambda o: copy_e(o).start())
    relocate(PACE[4])
    recv_e[e] = send_e[e]
    loads[9].wait()

    def first_half(o, carry):
        gate, upper, square = carry
        src = lax.rem(y + 4 - lax.div(o, 2), 4) * 2 + lax.rem(k + lax.rem(o, 2), 2)
        rows = recv_e[src].astype(F32)
        square = square + jnp.sum(rows * rows, axis=1, keepdims=True)
        gain = jnp.concatenate([gain_ref[pl.ds(6 * src + i, 1)] for i in range(6)], axis=1)
        scaled = (rows * gain).astype(BF16)
        start = pl.multiple_of(src * 768, 768)
        gate = gate + dot(scaled, win[0, pl.ds(start, 768)])
        upper = upper + dot(scaled, win[1, pl.ds(start, 768)])
        return gate, upper, square

    def arrived(o, carry):
        copy_e(o).wait_recv()
        return first_half(o, carry)

    zero = jnp.zeros((64, 256), F32)
    carry = first_half(0, (zero, zero, jnp.zeros((64, 1), F32)))
    gate, upper, square = lax.fori_loop(1, 8, arrived, carry)
    inverse = lax.rsqrt(square * (1.0 / 6144) + EPS)
    gate = gate * inverse
    act = (gate / (1.0 + jnp.exp(-gate)) * (upper * inverse)).astype(BF16)
    loads[10].wait()

    def copy_f(o):
        t = exp_at(lax.div(o, 2), lax.rem(o, 2))
        return remote(send_f.at[t], recv_f.at[e], sf.at[o], rf.at[o], exp=t)

    def second_half(t):
        start = pl.multiple_of(t * 768, 768)
        return (dot(act, wout[:, pl.ds(start, 768)]) * gate_col).astype(BF16)

    def produce(n):
        o = 8 - n
        t = exp_at(lax.div(o, 2), lax.rem(o, 2))
        send_f[t] = second_half(t)
        copy_f(o).start()

    loop(1, 8, produce)
    relocate(PACE[5])
    recv_f[e] = second_half(e)
    loop(1, 8, lambda o: copy_f(o).wait_recv())
    mixed = dot(selt[...], recv_f[...].reshape(512, 768))
    for dx in range(1, 4):
        send_g[dx] = mixed[32 * dx : 32 * dx + 32].astype(BF16)

    def copy_g(dx):
        return remote(send_g.at[dx], recv_g.at[dx], sg.at[dx], rg.at[dx], ctx=ctx_at(4 - dx, 0))

    def copy_h(dz):
        return remote(send_h.at[dz], recv_h.at[dz], sh.at[dz], rh.at[dz], ctx=ctx_at(0, 8 - dz))

    loop(1, 4, lambda dx: copy_g(dx).start())
    relocate(PACE[6])
    loop(1, 4, lambda dx: copy_g(dx).wait_recv())
    summed = mixed[0:32] + recv_g[1].astype(F32) + recv_g[2].astype(F32) + recv_g[3].astype(F32)
    cols = [summed[:, 128 * i : 128 * i + 128].reshape(4, 8, 128) for i in range(6)]
    sub4 = iota((4, 8, 128), 1)
    evens, odds = [], []
    for p in range(3):
        one, two = cols[2 * p], cols[2 * p + 1]
        evens.append(jnp.where(sub4 < 4, one, pltpu.roll(two, 4, 1)))
        odds.append(jnp.where(sub4 < 4, pltpu.roll(one, 4, 1), two))
    pad = [jnp.zeros((4, 8, 128), F32)]
    evens, odds = jnp.concatenate(evens + pad, axis=1), jnp.concatenate(odds + pad, axis=1)
    for n in range(4):
        send_h[2 * n] = evens[n].astype(BF16)
        send_h[2 * n + 1] = odds[n].astype(BF16)
    loop(1, 8, lambda dz: copy_h(dz).start())
    relocate(31)

    loop(1, 8, lambda dz: copy_h(dz).wait_recv())
    total = hidden + evens[0, 0:24]
    for dz in range(1, 8):
        total = total + recv_h[dz].astype(F32)[0:24]
    att_s[...] = total
    for i in range(6):
        lay_ref[:, 128 * i : 128 * i + 128] = att_s[4 * i : 4 * i + 4].astype(BF16)

    recv_r[0] = send_r[0]
    loop(1, 32, lambda o: copy_r(o, lax.div(o, 8), lax.rem(o, 8)).wait_recv())

    def place_block(s):
        block = recv_r[idxs[1, s]]
        fin_ref[:, s] = jnp.where(idxs[2, s] > 0, block, jnp.zeros_like(block))

    loop(0, 16, place_block)

    loop(1, 32, lambda o: copy_a(o).wait_send())
    loop(1, 8, lambda dz: copy_c(dz).wait_send())
    loop(1, 4, lambda dx: copy_d(dx).wait_send())
    loop(1, 8, lambda o: copy_e(o).wait_send())
    loop(1, 8, lambda o: copy_f(o).wait_send())
    loop(1, 4, lambda dx: copy_g(dx).wait_send())
    loop(1, 8, lambda dz: copy_h(dz).wait_send())
    loop(1, 32, lambda o: copy_r(o, lax.div(o, 8), lax.rem(o, 8)).wait_send())


def per_device(
    queries, new_kv, kv_cache, residual, kept_blocks, block_moves, expert_ids, gate_weights, norm_gain, expert_in,
    expert_out,
):
    vmem = pl.BlockSpec(memory_space=pltpu.VMEM)
    hbm = pl.BlockSpec(memory_space=pl.ANY)
    dma = pltpu.SemaphoreType.DMA
    layer, final = pl.pallas_call(
        kernel,
        out_shape=(
            jax.ShapeDtypeStruct((4, 768), BF16),
            jax.ShapeDtypeStruct((2, 16, 128, 128), BF16),
        ),
        in_specs=[hbm] * 11,
        out_specs=(vmem, vmem),
        scratch_shapes=[
            pltpu.VMEM((1, 512), I32),
            pltpu.VMEM((2, 4, 128), I32),
            pltpu.VMEM((2, 16, 128, 128), BF16),
            pltpu.VMEM((6, 128, 128), BF16),
            pltpu.VMEM((4, 2, 128), BF16),
            pltpu.VMEM((4, 768), BF16),
            pltpu.VMEM((2, 128), I32),
            pltpu.VMEM((2, 128), F32),
            pltpu.VMEM((48, 128), F32),
            pltpu.VMEM((2, 6144, 256), BF16),
            pltpu.VMEM((256, 6144), BF16),
            pltpu.VMEM((8, 128), I32),
            pltpu.SMEM((8, 128), I32),
            pltpu.VMEM((32, 32, 128), BF16),
            pltpu.VMEM((32, 32, 128), BF16),
            pltpu.VMEM((4, 8, 32, 128), BF16),
            pltpu.VMEM((8, 64, 768), BF16),
            pltpu.VMEM((8, 64, 768), BF16),
            pltpu.VMEM((8, 64, 768), BF16),
            pltpu.VMEM((8, 64, 768), BF16),
            pltpu.VMEM((4, 32, 768), BF16),
            pltpu.VMEM((4, 32, 768), BF16),
            pltpu.VMEM((8, 32, 128), BF16),
            pltpu.VMEM((8, 32, 128), BF16),
            pltpu.VMEM((32, 2, 128, 128), BF16),
            pltpu.VMEM((32, 2, 128, 128), BF16),
            pltpu.VMEM((8, 128), F32),
            pltpu.VMEM((8, 128), F32),
            pltpu.VMEM((8, 128), F32),
            pltpu.VMEM((8, 128), I32),
            pltpu.VMEM((8, 128), F32),
            pltpu.VMEM((128, 512), BF16),
            pltpu.VMEM((24, 128), F32),
            pltpu.VMEM((24, 128), F32),
            dma((12,)),
            dma((32,)), dma((32,)),
            dma((8,)), dma((8,)),
            dma((4,)), dma((4,)),
            dma((8,)), dma((8,)),
            dma((8,)), dma((8,)),
            dma((4,)), dma((4,)),
            dma((8,)), dma((8,)),
            dma((32,)), dma((32,)),
        ],
        compiler_params=pltpu.CompilerParams(
            collective_id=0, has_side_effects=True, vmem_limit_bytes=60 * 1024 * 1024
        ),
        name="layer",
    )(
        block_moves.reshape(1, 512),
        jnp.transpose(kept_blocks[:, 0], (0, 2, 1)),
        kv_cache.reshape(2, 16, 128, 128),
        jnp.transpose(queries[0], (1, 0, 2)),
        new_kv.reshape(4, 2, 128),
        residual.reshape(4, 768),
        expert_ids[0].T,
        gate_weights[0].T,
        norm_gain.reshape(48, 128),
        expert_in.reshape(2, 6144, 256),
        expert_out.reshape(256, 6144),
    )
    return layer.reshape(1, 4, 768), final.reshape(2, 1, 16, 128, 128)


def solution(mesh):
    in_specs = (
        P(None, None, "exp", None),
        P(None, "ctx", None, "exp", None),
        P(None, "exp", "ctx", None, None),
        P(None, "ctx", "exp"),
        P(None, "exp", None, None),
        P(None, "exp", None),
        P(),
        P(),
        P(),
        P("exp", None, None, "ctx"),
        P("exp", "ctx", None),
    )
    out_specs = (P(None, "ctx", "exp"), P(None, "exp", "ctx", None, None))
    return jax.shard_map(
        per_device, mesh=mesh, in_specs=in_specs, out_specs=out_specs, check_vma=False
    )
```

```python
import functools
import math

import jax
import jax.numpy as jnp
from jax import lax
from jax.experimental import pallas as pl
from jax.experimental.pallas import tpu as pltpu
from jax.sharding import PartitionSpec as P

MESH = pl.DeviceIdType.MESH
NEG = -1e30
EPS = 1e-05
F32, BF16, I32 = jnp.float32, jnp.bfloat16, jnp.int32

ORDER = tuple(
    (dx, dz)
    for dz in (0, 1, 7, 4, 3, 5, 2, 6)
    for dx in (2, 1, 3, 0)
    if (dx, dz) != (0, 0)
)
PACE = (5, 16, 10, 0, 0, 0, 0)


def iota(shape, dim):
    return lax.broadcasted_iota(I32, shape, dim)


def dot(a, b):
    return jnp.dot(a, b, preferred_element_type=F32)


def dot_nt(a, b):
    return lax.dot_general(a, b, (((1,), (1,)), ((), ())), preferred_element_type=F32)


def split3(v):
    first = v.astype(BF16).astype(F32)
    second = (v - first).astype(BF16).astype(F32)
    return first, second, v - first - second


def kernel(
    moves_hbm, kept_hbm, cache_hbm, q_hbm, nkv_hbm, res_hbm, ids_hbm, gates_hbm, gain_hbm, win_hbm, wout_hbm,
    lay_ref, recv_r, idxv,
    moves_ref, kept_ref, cache, q_ref, nkv_ref, res_ref, ids_ref, gates_ref, gain_ref, win, wout, idxs, send_a, recv_a, gx, send_e, recv_e, send_f, recv_f, send_g, recv_g, send_h, recv_h,
    send_r, scr, nks, nvs, slots, gatev, selt, att_s, res_s,
    lsem, sa, ra, sc, rc, sd, rd, se, re, sf, rf, sg, rg, sh, rh, sr, rr,
):
    c = lax.axis_index("ctx")
    e = lax.axis_index("exp")
    x, z = lax.div(c, 8), lax.rem(c, 8)
    y, k = lax.div(e, 2), lax.rem(e, 2)
    scale = 1.0 / math.sqrt(128)

    def ctx_at(dx, dz):
        return lax.rem(x + dx, 4) * 8 + lax.rem(z + dz, 8)

    def exp_at(dy, dk):
        return lax.rem(y + dy, 4) * 2 + lax.rem(k + dk, 2)

    def remote(src, dst, s, r, ctx=None, exp=None):
        return pltpu.make_async_remote_copy(
            src_ref=src, dst_ref=dst, send_sem=s, recv_sem=r,
            device_id=(c if ctx is None else ctx, e if exp is None else exp), device_id_type=MESH,
        )

    sources = (moves_hbm, kept_hbm, cache_hbm, q_hbm, nkv_hbm, res_hbm, ids_hbm, gates_hbm, gain_hbm, win_hbm, wout_hbm)
    targets = (moves_ref, kept_ref, cache, q_ref, nkv_ref, res_ref, ids_ref, gates_ref, gain_ref, win, wout)
    loads = [pltpu.make_async_copy(a, b, lsem.at[i]) for i, (a, b) in enumerate(zip(sources, targets))]
    for load in loads[:9]:
        load.start()

    barrier = pltpu.get_barrier_semaphore()

    def greet_ctx(o, carry):
        pl.semaphore_signal(
            barrier, inc=1, device_id=(ctx_at(lax.div(o, 8), lax.rem(o, 8)), e), device_id_type=MESH
        )
        return carry

    def greet_exp(o, carry):
        pl.semaphore_signal(
            barrier, inc=1, device_id=(c, exp_at(lax.div(o, 2), lax.rem(o, 2))), device_id_type=MESH
        )
        return carry

    lax.fori_loop(1, 32, greet_ctx, 0)
    lax.fori_loop(1, 8, greet_exp, 0)

    loads[0].wait()
    loads[1].wait()
    mv = moves_ref[...]
    lane = iota((32, 512), 1)
    off = iota((32, 512), 0)
    target = ((x + (off >> 3)) & 3) * 8 + ((z + (off & 7)) & 7)
    hit = ((mv >> 4) == target) & ((lane >> 4) == c)
    srcj = jnp.max(jnp.where(hit, lane & 15, 0), axis=1, keepdims=True)
    lane = iota((16, 512), 1)
    hit = mv == 16 * c + iota((16, 512), 0)
    place = ((x - (lane >> 7)) & 3) * 8 + ((z - ((lane >> 4) & 7)) & 7)
    rslot = jnp.max(jnp.where(hit, place, 0), axis=1, keepdims=True)
    kept1 = kept_ref[1]
    slot16 = 16 * c + iota((16, 128), 0)
    alive = kept1[0:1] == slot16
    for j in range(1, 4):
        alive = alive | (kept1[j : j + 1] == slot16)
    living = jnp.max(jnp.where(alive, 1, 0), axis=1, keepdims=True)
    eye32 = iota((32, 128), 0) == iota((32, 128), 1)
    eye16 = iota((16, 128), 0) == iota((16, 128), 1)
    idxv[0:1, :] = jnp.sum(jnp.where(eye32, srcj, 0), axis=0, keepdims=True)
    idxv[1:2, :] = jnp.sum(jnp.where(eye16, rslot, 0), axis=0, keepdims=True)
    idxv[2:3, :] = jnp.sum(jnp.where(eye16, living, 0), axis=0, keepdims=True)
    to_smem = pltpu.make_async_copy(idxv, idxs, lsem.at[11])
    to_smem.start()

    def copy_a(o):
        dx, dz = lax.div(o, 8), lax.rem(o, 8)
        t = ctx_at(dx, dz)
        return remote(send_a.at[t], recv_a.at[o], sa.at[o], ra.at[o], ctx=t)

    def copy_r(o, dx, dz):
        return remote(send_r.at[o], recv_r.at[o], sr.at[o], rr.at[o], ctx=ctx_at(dx, dz))

    done = [0]

    def relocate(count):
        for n in range(done[0], min(done[0] + count, len(ORDER))):
            dx, dz = ORDER[n]
            copy_r(dx * 8 + dz, dx, dz).start()
            done[0] = n + 1

    def loop(lo, hi, body):
        def step(o, carry):
            body(o)
            return carry

        lax.fori_loop(lo, hi, step, 0)

    rsub, rlane = iota((128, 128), 0), iota((128, 128), 1)
    kept0 = kept_ref[0]
    slot_id = 16 * c + (rsub & 15)
    owned = kept0[0:1] == slot_id
    for j in range(1, 4):
        owned = owned | (kept0[j : j + 1] == slot_id)
    owned = owned & (rsub < 96)
    ownf = jnp.where(owned, 1.0, 0.0)
    ownb = ownf.astype(BF16)
    owncol = jnp.sum(jnp.where(owned, rlane, 0), axis=1, keepdims=True)
    ownrow = dot_nt(iota((8, 128), 1).astype(F32).astype(BF16), ownb)[0:1].astype(I32)
    loads[3].wait()
    heads = [dot(ownb[16 * i : 16 * i + 16], q_ref[i]) for i in range(6)]
    q96 = jnp.concatenate(heads + [jnp.zeros((32, 128), F32)], axis=0).astype(BF16)
    loads[2].wait()
    loads[9].start()
    loads[10].start()
    scores = jnp.zeros((128, 128), F32)
    for j in range(16):
        scores = jnp.where((rsub & 15) == j, dot_nt(q96, cache[0, j]), scores)
    scores = scores * scale
    m = jnp.max(scores, axis=1, keepdims=True)
    probs = jnp.exp(scores - m).astype(BF16)
    l = jnp.sum(probs.astype(F32), axis=1, keepdims=True)
    out = jnp.zeros((128, 128), F32)
    for j in range(16):
        out = jnp.where((rsub & 15) == j, dot(probs, cache[1, j]), out)
    eye = rsub == rlane
    same = (owncol == ownrow) & ((rsub >> 4) == (rlane >> 4))
    mrow = jnp.sum(jnp.where(eye, m, 0.0), axis=0, keepdims=True)
    mseq = jnp.max(jnp.where(same, mrow, NEG), axis=1, keepdims=True)
    f = jnp.exp(m - mseq)
    lrow = jnp.sum(jnp.where(eye, l * f, 0.0), axis=0, keepdims=True)
    lseq = jnp.sum(jnp.where(same, lrow, 0.0), axis=1, keepdims=True)
    first = jnp.min(jnp.where(same, rlane.astype(F32), 999.0), axis=1, keepdims=True)
    place = ((rsub >> 4) << 2) + (owncol & 3)
    spread = (place == rlane) & (first == rsub.astype(F32)) & (rsub < 96)
    stats = [jnp.where(spread, v, 0.0).astype(BF16) for v in split3(mseq) + split3(lseq)]
    rl = iota((1, 128), 1)
    code = jnp.where(rl < 96, ((ownrow >> 2) << 5) + ((rl >> 4) << 2) + (ownrow & 3), -1)
    lift = jnp.where(iota((1024, 128), 0) == code, 1.0, 0.0).astype(BF16)
    values = dot(lift, (out * f).astype(BF16)).reshape(32, 32, 128)
    code = jnp.where(rl < 96, (ownrow >> 2) << 3, -100)
    row256 = iota((256, 128), 0)
    lift = jnp.concatenate([jnp.where(row256 == code + t, 1.0, 0.0).astype(BF16) for t in range(6)], axis=1)
    stat = dot(lift, jnp.concatenate(stats, axis=0)).reshape(32, 8, 128)
    send_a[...] = jnp.concatenate([values[:, 0:24], stat], axis=1).astype(BF16)

    pl.semaphore_wait(barrier, 38)
    loop(1, 32, lambda o: copy_a(o).start())
    recv_a[0] = send_a[c]

    to_smem.wait()

    def pack(o, carry):
        send_r[o] = cache[:, idxs[0, o]]
        return carry

    lax.fori_loop(0, 32, pack, 0)

    relocate(PACE[0])
    own_block = pltpu.make_async_copy(send_r.at[0], recv_r.at[0], lsem.at[12])
    own_block.start()

    for load in loads[4:9]:
        load.wait()
    res = res_ref[...].astype(F32)
    nks[0:4] = nkv_ref[:, 0].astype(F32)
    nks[4:8] = nkv_ref[:, 0].astype(F32)
    nvs[0:4] = nkv_ref[:, 1].astype(F32)
    nvs[4:8] = nkv_ref[:, 1].astype(F32)
    for i in range(6):
        res_s[4 * i : 4 * i + 4] = res[:, 128 * i : 128 * i + 128]
    s8, b8 = iota((8, 128), 0), iota((8, 128), 1)
    low = jnp.where((s8 < 4) & (b8 == 4 * c + s8), 1.0, 0.0).astype(BF16)
    high = jnp.where((s8 >= 4) & (b8 == 4 * c + s8 - 4), 1.0, 0.0).astype(BF16)
    q24 = jnp.concatenate([dot(low, q_ref[2 * p]) + dot(high, q_ref[2 * p + 1]) for p in range(3)], axis=0)
    nk24 = jnp.concatenate([nks[...]] * 3, axis=0)
    nv24 = jnp.concatenate([nvs[...]] * 3, axis=0)
    own_score = jnp.sum(q24 * nk24, axis=1, keepdims=True) * scale
    eye24 = iota((24, 128), 0) == iota((24, 128), 1)
    own_score = jnp.sum(jnp.where(eye24, own_score, 0.0), axis=0, keepdims=True)

    g3 = split3(gates_ref[...])
    scr[0:2] = ids_ref[...].astype(F32)
    for i in range(3):
        scr[2 * i + 2 : 2 * i + 4] = g3[i]
    o128 = rlane >> 2
    group = ((x - (o128 >> 3)) & 3) * 8 + ((z - (o128 & 7)) & 7)
    relative = jnp.where(rsub == 4 * group + (rlane & 3), 1.0, 0.0).astype(BF16)
    routed = dot(scr[...].astype(BF16), relative)
    r0, r1 = routed[0:1].astype(I32), routed[1:2].astype(I32)
    w0 = routed[2:3] + routed[4:5] + routed[6:7]
    w1 = routed[3:4] + routed[5:6] + routed[7:8]
    goes = jnp.where((r0 == s8) | (r1 == s8), 1, 0)
    rank = jnp.zeros((8, 128), I32)
    for d in range(1, 4):
        rank = rank + jnp.where((b8 & 3) >= d, pltpu.roll(goes, d, 1), 0)
    slot = jnp.where(goes > 0, ((b8 >> 2) << 1) + rank, -1)
    slots[...] = slot
    gatev[...] = jnp.where(r0 == s8, w0, 0.0) + jnp.where(r1 == s8, w1, 0.0)
    row64 = iota((64, 128), 0)
    sel = jnp.concatenate([jnp.where(row64 == slot[j : j + 1], 1.0, 0.0) for j in range(8)], axis=0)
    selt[...] = sel.T.astype(BF16)
    sel = sel.astype(BF16)
    gate_col = jnp.sum(
        jnp.where(row64 == slots[pl.ds(e, 1)], gatev[pl.ds(e, 1)], 0.0), axis=1, keepdims=True
    )

    loop(1, 32, lambda o: copy_a(o).wait_recv())
    got = recv_a[...].astype(F32)
    st = got[:, 24:32]
    qi = iota((32, 8, 128), 1)
    m = jnp.sum(jnp.where(qi < 3, st, 0.0), axis=1, keepdims=True)
    l = jnp.sum(jnp.where((qi >= 3) & (qi < 6), st, 0.0), axis=1, keepdims=True)
    m = jnp.where(l > 0, m, NEG)
    top = jnp.maximum(jnp.max(m, axis=0), own_score)
    w = jnp.where(l > 0, jnp.exp(m - top[None]), 0.0)
    fresh = jnp.exp(own_score - top)
    inv_den = 1.0 / (jnp.sum(w * l, axis=0) + fresh)
    w = w * inv_den[None]
    wcol = jnp.sum(jnp.where(eye24[None], jnp.broadcast_to(w, (32, 24, 128)), 0.0), axis=2, keepdims=True)
    att = jnp.sum(wcol * got[:, 0:24], axis=0)
    fcol = jnp.sum(jnp.where(eye24, fresh * inv_den, 0.0), axis=1, keepdims=True)
    att = att + fcol * nv24
    hidden = (res_s[...] + att).astype(BF16).astype(F32)
    gx[0, 0] = jnp.concatenate([hidden, jnp.zeros((8, 128), F32)], axis=0).astype(BF16)

    def copy_c(dz):
        return remote(gx.at[0, 0], gx.at[0, dz], sc.at[dz], rc.at[dz], ctx=ctx_at(0, dz))

    def copy_d(dx):
        return remote(gx.at[0], gx.at[dx], sd.at[dx], rd.at[dx], ctx=ctx_at(dx, 0))

    loop(1, 8, lambda dz: copy_c(dz).start())
    relocate(PACE[1])
    loop(1, 8, lambda dz: copy_c(dz).wait_recv())
    loop(1, 4, lambda dx: copy_d(dx).start())
    relocate(PACE[2])
    loop(1, 4, lambda dx: copy_d(dx).wait_recv())

    flat = gx[...].reshape(32, 32, 128).astype(F32).reshape(16, 2, 32, 128)
    sub16 = iota((16, 8, 128), 1)
    parts = []
    for p in range(3):
        one, two = flat[:, 0, 8 * p : 8 * p + 8], flat[:, 1, 8 * p : 8 * p + 8]
        parts.append(jnp.where(sub16 < 4, one, pltpu.roll(two, 4, 1)).reshape(128, 128).astype(BF16))
        parts.append(jnp.where(sub16 < 4, pltpu.roll(one, 4, 1), two).reshape(128, 128).astype(BF16))
    tokens = jnp.concatenate(parts, axis=1)

    def copy_e(o):
        t = exp_at(lax.div(o, 2), lax.rem(o, 2))
        return remote(send_e.at[t], recv_e.at[e], se.at[o], re.at[o], exp=t)

    for j in range(8):
        send_e[j] = dot(sel[64 * j : 64 * j + 64], tokens).astype(BF16)
    loop(1, 8, lambda o: copy_e(o).start())
    relocate(PACE[3])
    recv_e[e] = send_e[e]
    loads[9].wait()

    def first_half(o, carry):
        gate, upper, square = carry
        src = lax.rem(y + 4 - lax.div(o, 2), 4) * 2 + lax.rem(k + lax.rem(o, 2), 2)
        rows = recv_e[src].astype(F32)
        square = square + jnp.sum(rows * rows, axis=1, keepdims=True)
        gain = jnp.concatenate([gain_ref[pl.ds(6 * src + i, 1)] for i in range(6)], axis=1)
        scaled = (rows * gain).astype(BF16)
        start = pl.multiple_of(src * 768, 768)
        gate = gate + dot(scaled, win[0, pl.ds(start, 768)])
        upper = upper + dot(scaled, win[1, pl.ds(start, 768)])
        return gate, upper, square

    def arrived(o, carry):
        copy_e(o).wait_recv()
        return first_half(o, carry)

    zero = jnp.zeros((64, 256), F32)
    carry = first_half(0, (zero, zero, jnp.zeros((64, 1), F32)))
    gate, upper, square = lax.fori_loop(1, 8, arrived, carry)
    inverse = lax.rsqrt(square * (1.0 / 6144) + EPS)
    gate = gate * inverse
    act = (gate / (1.0 + jnp.exp(-gate)) * (upper * inverse)).astype(BF16)
    loads[10].wait()

    def copy_f(o):
        t = exp_at(lax.div(o, 2), lax.rem(o, 2))
        return remote(send_f.at[t], recv_f.at[e], sf.at[o], rf.at[o], exp=t)

    def second_half(t):
        start = pl.multiple_of(t * 768, 768)
        return (dot(act, wout[:, pl.ds(start, 768)]) * gate_col).astype(BF16)

    def produce(n):
        o = 8 - n
        t = exp_at(lax.div(o, 2), lax.rem(o, 2))
        send_f[t] = second_half(t)
        copy_f(o).start()

    loop(1, 8, produce)
    relocate(PACE[4])
    recv_f[e] = second_half(e)
    loop(1, 8, lambda o: copy_f(o).wait_recv())
    mixed = dot(selt[...], recv_f[...].reshape(512, 768))
    for dx in range(1, 4):
        send_g[dx] = mixed[32 * dx : 32 * dx + 32].astype(BF16)

    def copy_g(dx):
        return remote(send_g.at[dx], recv_g.at[dx], sg.at[dx], rg.at[dx], ctx=ctx_at(4 - dx, 0))

    def copy_h(dz):
        return remote(send_h.at[dz], recv_h.at[dz], sh.at[dz], rh.at[dz], ctx=ctx_at(0, 8 - dz))

    loop(1, 4, lambda dx: copy_g(dx).start())
    relocate(PACE[5])
    loop(1, 4, lambda dx: copy_g(dx).wait_recv())
    summed = mixed[0:32] + recv_g[1].astype(F32) + recv_g[2].astype(F32) + recv_g[3].astype(F32)
    cols = [summed[:, 128 * i : 128 * i + 128].reshape(4, 8, 128) for i in range(6)]
    sub4 = iota((4, 8, 128), 1)
    evens, odds = [], []
    for p in range(3):
        one, two = cols[2 * p], cols[2 * p + 1]
        evens.append(jnp.where(sub4 < 4, one, pltpu.roll(two, 4, 1)))
        odds.append(jnp.where(sub4 < 4, pltpu.roll(one, 4, 1), two))
    pad = [jnp.zeros((4, 8, 128), F32)]
    evens, odds = jnp.concatenate(evens + pad, axis=1), jnp.concatenate(odds + pad, axis=1)
    for n in range(4):
        send_h[2 * n] = evens[n].astype(BF16)
        send_h[2 * n + 1] = odds[n].astype(BF16)
    loop(1, 8, lambda dz: copy_h(dz).start())
    relocate(31)

    loop(1, 8, lambda dz: copy_h(dz).wait_recv())
    total = hidden + evens[0, 0:24]
    for dz in range(1, 8):
        total = total + recv_h[dz].astype(F32)[0:24]
    att_s[...] = total
    for i in range(6):
        lay_ref[:, 128 * i : 128 * i + 128] = att_s[4 * i : 4 * i + 4].astype(BF16)

    own_block.wait()
    loop(1, 32, lambda o: copy_r(o, lax.div(o, 8), lax.rem(o, 8)).wait_recv())
    loop(1, 32, lambda o: copy_a(o).wait_send())
    loop(1, 8, lambda dz: copy_c(dz).wait_send())
    loop(1, 4, lambda dx: copy_d(dx).wait_send())
    loop(1, 8, lambda o: copy_e(o).wait_send())
    loop(1, 8, lambda o: copy_f(o).wait_send())
    loop(1, 4, lambda dx: copy_g(dx).wait_send())
    loop(1, 8, lambda dz: copy_h(dz).wait_send())
    loop(1, 32, lambda o: copy_r(o, lax.div(o, 8), lax.rem(o, 8)).wait_send())


def place_blocks(idxs, layer_hbm, blocks_hbm, lay_hbm, fin_hbm, zeros, sem):
    last = pltpu.make_async_copy(layer_hbm, lay_hbm, sem.at[16])
    last.start()
    zeros[...] = jnp.zeros_like(zeros)

    def start(s, carry):
        @pl.when(idxs[2, s] > 0)
        def _():
            pltpu.make_async_copy(blocks_hbm.at[idxs[1, s]], fin_hbm.at[:, s], sem.at[s]).start()

        @pl.when(idxs[2, s] == 0)
        def _():
            pltpu.make_async_copy(zeros, fin_hbm.at[:, s], sem.at[s]).start()

        return carry

    def wait(s, carry):
        pltpu.make_async_copy(zeros, fin_hbm.at[:, s], sem.at[s]).wait()
        return carry

    lax.fori_loop(0, 16, start, 0)
    lax.fori_loop(0, 16, wait, 0)
    last.wait()


def per_device(
    queries, new_kv, kv_cache, residual, kept_blocks, block_moves, expert_ids, gate_weights, norm_gain, expert_in,
    expert_out,
):
    vmem = pl.BlockSpec(memory_space=pltpu.VMEM)
    hbm = pl.BlockSpec(memory_space=pl.ANY)
    dma = pltpu.SemaphoreType.DMA
    layer, blocks, index = pl.pallas_call(
        kernel,
        out_shape=(
            jax.ShapeDtypeStruct((4, 768), BF16),
            jax.ShapeDtypeStruct((32, 2, 128, 128), BF16),
            jax.ShapeDtypeStruct((8, 128), I32),
        ),
        in_specs=[hbm] * 11,
        out_specs=(vmem, hbm, vmem),
        scratch_shapes=[
            pltpu.VMEM((1, 512), I32),
            pltpu.VMEM((2, 4, 128), I32),
            pltpu.VMEM((2, 16, 128, 128), BF16),
            pltpu.VMEM((6, 128, 128), BF16),
            pltpu.VMEM((4, 2, 128), BF16),
            pltpu.VMEM((4, 768), BF16),
            pltpu.VMEM((2, 128), I32),
            pltpu.VMEM((2, 128), F32),
            pltpu.VMEM((48, 128), F32),
            pltpu.VMEM((2, 6144, 256), BF16),
            pltpu.VMEM((256, 6144), BF16),
            pltpu.SMEM((8, 128), I32),
            pltpu.VMEM((32, 32, 128), BF16),
            pltpu.VMEM((32, 32, 128), BF16),
            pltpu.VMEM((4, 8, 32, 128), BF16),
            pltpu.VMEM((8, 64, 768), BF16),
            pltpu.VMEM((8, 64, 768), BF16),
            pltpu.VMEM((8, 64, 768), BF16),
            pltpu.VMEM((8, 64, 768), BF16),
            pltpu.VMEM((4, 32, 768), BF16),
            pltpu.VMEM((4, 32, 768), BF16),
            pltpu.VMEM((8, 32, 128), BF16),
            pltpu.VMEM((8, 32, 128), BF16),
            pltpu.VMEM((32, 2, 128, 128), BF16),
            pltpu.VMEM((8, 128), F32),
            pltpu.VMEM((8, 128), F32),
            pltpu.VMEM((8, 128), F32),
            pltpu.VMEM((8, 128), I32),
            pltpu.VMEM((8, 128), F32),
            pltpu.VMEM((128, 512), BF16),
            pltpu.VMEM((24, 128), F32),
            pltpu.VMEM((24, 128), F32),
            dma((13,)),
            dma((32,)), dma((32,)),
            dma((8,)), dma((8,)),
            dma((4,)), dma((4,)),
            dma((8,)), dma((8,)),
            dma((8,)), dma((8,)),
            dma((4,)), dma((4,)),
            dma((8,)), dma((8,)),
            dma((32,)), dma((32,)),
        ],
        compiler_params=pltpu.CompilerParams(
            collective_id=0, has_side_effects=True, vmem_limit_bytes=60 * 1024 * 1024
        ),
        name="layer",
    )(
        block_moves.reshape(1, 512),
        jnp.transpose(kept_blocks[:, 0], (0, 2, 1)),
        kv_cache.reshape(2, 16, 128, 128),
        jnp.transpose(queries[0], (1, 0, 2)),
        new_kv.reshape(4, 2, 128),
        residual.reshape(4, 768),
        expert_ids[0].T,
        gate_weights[0].T,
        norm_gain.reshape(48, 128),
        expert_in.reshape(2, 6144, 256),
        expert_out.reshape(256, 6144),
    )
    layer, final = pl.pallas_call(
        place_blocks,
        out_shape=(
            jax.ShapeDtypeStruct((4, 768), BF16),
            jax.ShapeDtypeStruct((2, 16, 128, 128), BF16),
        ),
        in_specs=[pl.BlockSpec(memory_space=pltpu.SMEM), hbm, hbm],
        out_specs=(hbm, hbm),
        scratch_shapes=[pltpu.VMEM((2, 128, 128), BF16), dma((17,))],
        compiler_params=pltpu.CompilerParams(vmem_limit_bytes=60 * 1024 * 1024),
        name="place_blocks",
    )(index, layer, blocks)
    return layer.reshape(1, 4, 768), final.reshape(2, 1, 16, 128, 128)


def solution(mesh):
    in_specs = (
        P(None, None, "exp", None),
        P(None, "ctx", None, "exp", None),
        P(None, "exp", "ctx", None, None),
        P(None, "ctx", "exp"),
        P(None, "exp", None, None),
        P(None, "exp", None),
        P(),
        P(),
        P(),
        P("exp", None, None, "ctx"),
        P("exp", "ctx", None),
    )
    out_specs = (P(None, "ctx", "exp"), P(None, "exp", "ctx", None, None))
    return jax.shard_map(
        per_device, mesh=mesh, in_specs=in_specs, out_specs=out_specs, check_vma=False
    )
```

```python
import functools
import math

import jax
import jax.numpy as jnp
from jax import lax
from jax.experimental import pallas as pl
from jax.experimental.pallas import tpu as pltpu
from jax.sharding import PartitionSpec as P

MESH = pl.DeviceIdType.MESH
NEG = -1e30
EPS = 1e-05
F32, BF16, I32 = jnp.float32, jnp.bfloat16, jnp.int32

def along_z(*dzs):
    return tuple((0, dz) for dz in dzs)


def mixed_with(*dzs):
    return tuple((dx, dz) for dz in dzs for dx in (2, 1, 3))


ALONG_X = ((2, 0), (1, 0), (3, 0))
STAGES = (
    along_z(1, 7),
    ALONG_X,
    along_z(2, 6, 3, 5, 4),
    mixed_with(4, 3, 5),
    mixed_with(2, 6, 1, 7),
    (),
    (),
    (),
)


def iota(shape, dim):
    return lax.broadcasted_iota(I32, shape, dim)


def dot(a, b):
    return jnp.dot(a, b, preferred_element_type=F32)


def dot_nt(a, b):
    return lax.dot_general(a, b, (((1,), (1,)), ((), ())), preferred_element_type=F32)


def split3(v):
    first = v.astype(BF16).astype(F32)
    second = (v - first).astype(BF16).astype(F32)
    return first, second, v - first - second


def kernel(
    moves_hbm, kept_hbm, cache_hbm, q_hbm, nkv_hbm, res_hbm, ids_hbm, gates_hbm, gain_hbm, win_hbm, wout_hbm,
    lay_ref, recv_r, idxv,
    moves_ref, kept_ref, cache, q_ref, nkv_ref, res_ref, ids_ref, gates_ref, gain_ref, win, wout, idxs,
    send_a, recv_a, send_b, recv_b, gx, send_e, recv_e, send_f, recv_f, send_n, recv_n, send_g, recv_g, send_h, recv_h,
    send_r, scr, nks, nvs, slots, gatev, sel_far, sel_near, att_s, res_s,
    lsem, sa, ra, sb, rb, sc, rc, sd, rd, se, re, sf, rf, sn, rn, sg, rg, sh, rh, sr, rr,
):
    c = lax.axis_index("ctx")
    e = lax.axis_index("exp")
    x, z = lax.div(c, 8), lax.rem(c, 8)
    y, k = lax.div(e, 2), lax.rem(e, 2)
    scale = 1.0 / math.sqrt(128)

    def ctx_at(dx, dz):
        return lax.rem(x + dx, 4) * 8 + lax.rem(z + dz, 8)

    def exp_at(dy, dk):
        return lax.rem(y + dy, 4) * 2 + lax.rem(k + dk, 2)

    def remote(src, dst, s, r, ctx=None, exp=None):
        return pltpu.make_async_remote_copy(
            src_ref=src, dst_ref=dst, send_sem=s, recv_sem=r,
            device_id=(c if ctx is None else ctx, e if exp is None else exp), device_id_type=MESH,
        )

    sources = (moves_hbm, kept_hbm, cache_hbm, q_hbm, nkv_hbm, res_hbm, ids_hbm, gates_hbm, gain_hbm, win_hbm, wout_hbm)
    targets = (moves_ref, kept_ref, cache, q_ref, nkv_ref, res_ref, ids_ref, gates_ref, gain_ref, win, wout)
    loads = [pltpu.make_async_copy(a, b, lsem.at[i]) for i, (a, b) in enumerate(zip(sources, targets))]
    for load in loads[:9]:
        load.start()

    barrier = pltpu.get_barrier_semaphore()

    def greet_ctx(o, carry):
        pl.semaphore_signal(
            barrier, inc=1, device_id=(ctx_at(lax.div(o, 8), lax.rem(o, 8)), e), device_id_type=MESH
        )
        return carry

    def greet_exp(o, carry):
        pl.semaphore_signal(
            barrier, inc=1, device_id=(c, exp_at(lax.div(o, 2), lax.rem(o, 2))), device_id_type=MESH
        )
        return carry

    lax.fori_loop(1, 32, greet_ctx, 0)
    lax.fori_loop(1, 8, greet_exp, 0)

    loads[0].wait()
    loads[1].wait()
    mv = moves_ref[...]
    lane = iota((32, 512), 1)
    off = iota((32, 512), 0)
    target = ((x + (off >> 3)) & 3) * 8 + ((z + (off & 7)) & 7)
    hit = ((mv >> 4) == target) & ((lane >> 4) == c)
    srcj = jnp.max(jnp.where(hit, lane & 15, 0), axis=1, keepdims=True)
    lane = iota((16, 512), 1)
    hit = mv == 16 * c + iota((16, 512), 0)
    place = ((x - (lane >> 7)) & 3) * 8 + ((z - ((lane >> 4) & 7)) & 7)
    rslot = jnp.max(jnp.where(hit, place, 0), axis=1, keepdims=True)
    kept1 = kept_ref[1]
    slot16 = 16 * c + iota((16, 128), 0)
    alive = kept1[0:1] == slot16
    for j in range(1, 4):
        alive = alive | (kept1[j : j + 1] == slot16)
    living = jnp.max(jnp.where(alive, 1, 0), axis=1, keepdims=True)
    eye32 = iota((32, 128), 0) == iota((32, 128), 1)
    eye16 = iota((16, 128), 0) == iota((16, 128), 1)
    idxv[0:1, :] = jnp.sum(jnp.where(eye32, srcj, 0), axis=0, keepdims=True)
    idxv[1:2, :] = jnp.sum(jnp.where(eye16, rslot, 0), axis=0, keepdims=True)
    idxv[2:3, :] = jnp.sum(jnp.where(eye16, living, 0), axis=0, keepdims=True)
    to_smem = pltpu.make_async_copy(idxv, idxs, lsem.at[11])
    to_smem.start()

    def copy_a(dx):
        row = lax.rem(x + dx, 4)
        return remote(send_a.at[row], recv_a.at[dx], sa.at[dx], ra.at[dx], ctx=row * 8 + z)

    def copy_b(dz):
        to = lax.rem(z + dz, 8)
        return remote(send_b.at[to], recv_b.at[dz], sb.at[dz], rb.at[dz], ctx=x * 8 + to)

    def copy_r(o, dx, dz):
        return remote(send_r.at[o], recv_r.at[o], sr.at[o], rr.at[o], ctx=ctx_at(dx, dz))

    def relocate(stage):
        for dx, dz in STAGES[stage]:
            copy_r(dx * 8 + dz, dx, dz).start()

    def loop(lo, hi, body):
        def step(o, carry):
            body(o)
            return carry

        lax.fori_loop(lo, hi, step, 0)

    rsub, rlane = iota((128, 128), 0), iota((128, 128), 1)
    kept0 = kept_ref[0]
    slot_id = 16 * c + (rsub & 15)
    owned = kept0[0:1] == slot_id
    for j in range(1, 4):
        owned = owned | (kept0[j : j + 1] == slot_id)
    owned = owned & (rsub < 96)
    ownf = jnp.where(owned, 1.0, 0.0)
    ownb = ownf.astype(BF16)
    owncol = jnp.sum(jnp.where(owned, rlane, 0), axis=1, keepdims=True)
    ownrow = dot_nt(iota((8, 128), 1).astype(F32).astype(BF16), ownb)[0:1].astype(I32)
    loads[3].wait()
    heads = [dot(ownb[16 * i : 16 * i + 16], q_ref[i]) for i in range(6)]
    q96 = jnp.concatenate(heads + [jnp.zeros((32, 128), F32)], axis=0).astype(BF16)
    loads[2].wait()
    loads[9].start()
    loads[10].start()
    scores = jnp.zeros((128, 128), F32)
    for j in range(16):
        scores = jnp.where((rsub & 15) == j, dot_nt(q96, cache[0, j]), scores)
    scores = scores * scale
    m = jnp.max(scores, axis=1, keepdims=True)
    probs = jnp.exp(scores - m).astype(BF16)
    l = jnp.sum(probs.astype(F32), axis=1, keepdims=True)
    out = jnp.zeros((128, 128), F32)
    for j in range(16):
        out = jnp.where((rsub & 15) == j, dot(probs, cache[1, j]), out)
    eye = rsub == rlane
    same = (owncol == ownrow) & ((rsub >> 4) == (rlane >> 4))
    mrow = jnp.sum(jnp.where(eye, m, 0.0), axis=0, keepdims=True)
    mseq = jnp.max(jnp.where(same, mrow, NEG), axis=1, keepdims=True)
    f = jnp.exp(m - mseq)
    lrow = jnp.sum(jnp.where(eye, l * f, 0.0), axis=0, keepdims=True)
    lseq = jnp.sum(jnp.where(same, lrow, 0.0), axis=1, keepdims=True)
    first = jnp.min(jnp.where(same, rlane.astype(F32), 999.0), axis=1, keepdims=True)
    place = ((rsub >> 4) << 2) + (owncol & 3)
    spread = (place == rlane) & (first == rsub.astype(F32)) & (rsub < 96)
    stats = [jnp.where(spread, v, 0.0).astype(BF16) for v in split3(mseq) + split3(lseq)]
    rl = iota((1, 128), 1)
    code = jnp.where(rl < 96, ((ownrow >> 2) << 5) + ((rl >> 4) << 2) + (ownrow & 3), -1)
    lift = jnp.where(iota((1024, 128), 0) == code, 1.0, 0.0).astype(BF16)
    values = dot(lift, (out * f).astype(BF16)).reshape(32, 32, 128)
    code = jnp.where(rl < 96, (ownrow >> 2) << 3, -100)
    row256 = iota((256, 128), 0)
    lift = jnp.concatenate([jnp.where(row256 == code + t, 1.0, 0.0).astype(BF16) for t in range(6)], axis=1)
    stat = dot(lift, jnp.concatenate(stats, axis=0)).reshape(32, 8, 128)
    send_a[...] = jnp.concatenate([values[:, 0:24], stat], axis=1).astype(BF16).reshape(4, 8, 32, 128)

    pl.semaphore_wait(barrier, 38)
    loop(1, 4, lambda dx: copy_a(dx).start())
    recv_a[0] = send_a[x]

    to_smem.wait()

    def pack(o, carry):
        send_r[o] = cache[:, idxs[0, o]]
        return carry

    lax.fori_loop(0, 32, pack, 0)

    relocate(0)
    own_block = pltpu.make_async_copy(send_r.at[0], recv_r.at[0], lsem.at[12])
    own_block.start()

    for load in loads[4:9]:
        load.wait()
    res = res_ref[...].astype(F32)
    nks[0:4] = nkv_ref[:, 0].astype(F32)
    nks[4:8] = nkv_ref[:, 0].astype(F32)
    nvs[0:4] = nkv_ref[:, 1].astype(F32)
    nvs[4:8] = nkv_ref[:, 1].astype(F32)
    for i in range(6):
        res_s[4 * i : 4 * i + 4] = res[:, 128 * i : 128 * i + 128]
    s8, b8 = iota((8, 128), 0), iota((8, 128), 1)
    low = jnp.where((s8 < 4) & (b8 == 4 * c + s8), 1.0, 0.0).astype(BF16)
    high = jnp.where((s8 >= 4) & (b8 == 4 * c + s8 - 4), 1.0, 0.0).astype(BF16)
    q24 = jnp.concatenate([dot(low, q_ref[2 * p]) + dot(high, q_ref[2 * p + 1]) for p in range(3)], axis=0)
    nk24 = jnp.concatenate([nks[...]] * 3, axis=0)
    nv24 = jnp.concatenate([nvs[...]] * 3, axis=0)
    own_score = jnp.sum(q24 * nk24, axis=1, keepdims=True) * scale
    eye24 = iota((24, 128), 0) == iota((24, 128), 1)
    own_score = jnp.sum(jnp.where(eye24, own_score, 0.0), axis=0, keepdims=True)

    g3 = split3(gates_ref[...])
    scr[0:2] = ids_ref[...].astype(F32)
    for i in range(3):
        scr[2 * i + 2 : 2 * i + 4] = g3[i]
    o128 = rlane >> 2
    group = ((x - (o128 >> 3)) & 3) * 8 + ((z - (o128 & 7)) & 7)
    relative = jnp.where(rsub == 4 * group + (rlane & 3), 1.0, 0.0).astype(BF16)
    routed = dot(scr[...].astype(BF16), relative)
    r0, r1 = routed[0:1].astype(I32), routed[1:2].astype(I32)
    w0 = routed[2:3] + routed[4:5] + routed[6:7]
    w1 = routed[3:4] + routed[5:6] + routed[7:8]
    goes = jnp.where((r0 == s8) | (r1 == s8), 1, 0)
    rank = jnp.zeros((8, 128), I32)
    for d in range(1, 4):
        rank = rank + jnp.where((b8 & 3) >= d, pltpu.roll(goes, d, 1), 0)
    slot = jnp.where(goes > 0, ((b8 >> 2) << 1) + rank, -1)
    slots[...] = slot
    gatev[...] = jnp.where(r0 == s8, w0, 0.0) + jnp.where(r1 == s8, w1, 0.0)
    row64 = iota((64, 128), 0)
    sel = jnp.concatenate([jnp.where(row64 == slot[j : j + 1], 1.0, 0.0) for j in range(8)], axis=0)
    picks = []
    for dx in range(4):
        block = jnp.concatenate([sel[64 * j + 16 * dx : 64 * j + 16 * dx + 16] for j in range(8)], axis=0)
        if dx:
            block = pltpu.roll(block, 128 - 32 * dx, 1)
        picks.append(block[:, 0:32].astype(BF16))
    far_rows = jnp.concatenate([sel[64 * j + 16 : 64 * j + 64] for j in range(8)], axis=0).T
    near_rows = jnp.concatenate([sel[64 * j : 64 * j + 16] for j in range(8)], axis=0).T
    sel_far[...] = far_rows[32:128].astype(BF16)
    sel_near[...] = near_rows[0:32].astype(BF16)
    gate_col = jnp.sum(
        jnp.where(row64 == slots[pl.ds(e, 1)], gatev[pl.ds(e, 1)], 0.0), axis=1, keepdims=True
    )

    def unpack(got):
        st = got[:, 24:32]
        qi = iota(st.shape, 1)
        m = jnp.sum(jnp.where(qi < 3, st, 0.0), axis=1, keepdims=True)
        l = jnp.sum(jnp.where((qi >= 3) & (qi < 6), st, 0.0), axis=1, keepdims=True)
        return jnp.where(l > 0, m, NEG), l

    def column(w):
        wide = jnp.broadcast_to(w, (w.shape[0], 24, 128))
        return jnp.sum(jnp.where(eye24[None], wide, 0.0), axis=2, keepdims=True)

    loop(1, 4, lambda dx: copy_a(dx).wait_recv())
    got = recv_a[...].astype(F32).reshape(32, 32, 128)
    m, l = unpack(got)
    m, l = m.reshape(4, 8, 1, 128), l.reshape(4, 8, 1, 128)
    top = jnp.max(m, axis=0)
    w = jnp.where(l > 0, jnp.exp(m - top[None]), 0.0)
    l = jnp.sum(w * l, axis=0)
    parts = split3(jnp.where(l > 0, top, 0.0)) + split3(l)
    qi = iota((8, 8, 128), 1)
    stat = jnp.zeros((8, 8, 128), F32)
    for n in range(6):
        stat = jnp.where(qi == n, parts[n], stat)
    values = column(w.reshape(32, 1, 128)) * got[:, 0:24]
    values = jnp.sum(values.reshape(4, 8, 24, 128), axis=0)
    send_b[...] = jnp.concatenate([values, stat], axis=1).astype(BF16)
    loop(1, 8, lambda dz: copy_b(dz).start())
    recv_b[0] = send_b[z]
    relocate(1)
    loop(1, 8, lambda dz: copy_b(dz).wait_recv())
    got = recv_b[...].astype(F32)
    m, l = unpack(got)
    top = jnp.maximum(jnp.max(m, axis=0), own_score)
    w = jnp.where(l > 0, jnp.exp(m - top[None]), 0.0)
    fresh = jnp.exp(own_score - top)
    inv_den = 1.0 / (jnp.sum(w * l, axis=0) + fresh)
    att = jnp.sum(column(w * inv_den[None]) * got[:, 0:24], axis=0)
    fcol = jnp.sum(jnp.where(eye24, fresh * inv_den, 0.0), axis=1, keepdims=True)
    att = att + fcol * nv24
    hidden = (res_s[...] + att).astype(BF16).astype(F32)
    gx[0, 0] = jnp.concatenate([hidden, jnp.zeros((8, 128), F32)], axis=0).astype(BF16)

    def copy_c(dz):
        return remote(gx.at[0, 0], gx.at[0, dz], sc.at[dz], rc.at[dz], ctx=ctx_at(0, dz))

    def copy_d(dx):
        return remote(gx.at[0], gx.at[dx], sd.at[dx], rd.at[dx], ctx=ctx_at(dx, 0))

    def copy_e(dx, o):
        t = exp_at(lax.div(o, 2), lax.rem(o, 2))
        rows = pl.ds(16 * dx, 16)
        return remote(send_e.at[t, rows], recv_e.at[e, rows], se.at[8 * dx + o], re.at[8 * dx + o], exp=t)

    def dispatch(dx):
        flat = gx[dx].astype(F32).reshape(4, 2, 32, 128)
        parts = []
        for p in range(3):
            one, two = flat[:, 0, 8 * p : 8 * p + 8], flat[:, 1, 8 * p : 8 * p + 8]
            parts.append(jnp.where(sub4 < 4, one, pltpu.roll(two, 4, 1)).reshape(32, 128).astype(BF16))
            parts.append(jnp.where(sub4 < 4, pltpu.roll(one, 4, 1), two).reshape(32, 128).astype(BF16))
        rows = dot(picks[dx], jnp.concatenate(parts, axis=1)).astype(BF16)
        for j in range(8):
            send_e[j, 16 * dx : 16 * dx + 16] = rows[16 * j : 16 * j + 16]
        loop(1, 8, lambda o: copy_e(dx, o).start())

    sub4 = iota((4, 8, 128), 1)
    loop(1, 8, lambda dz: copy_c(dz).start())
    relocate(2)
    loop(1, 8, lambda dz: copy_c(dz).wait_recv())
    loop(1, 4, lambda dx: copy_d(dx).start())
    dispatch(0)
    relocate(3)
    for dx in (1, 3, 2):
        copy_d(dx).wait_recv()
        dispatch(dx)
    relocate(4)
    recv_e[e] = send_e[e]
    loads[9].wait()

    def first_half(o, carry):
        gate, upper, square = carry
        src = lax.rem(y + 4 - lax.div(o, 2), 4) * 2 + lax.rem(k + lax.rem(o, 2), 2)
        rows = recv_e[src].astype(F32)
        square = square + jnp.sum(rows * rows, axis=1, keepdims=True)
        gain = jnp.concatenate([gain_ref[pl.ds(6 * src + i, 1)] for i in range(6)], axis=1)
        scaled = (rows * gain).astype(BF16)
        start = pl.multiple_of(src * 768, 768)
        gate = gate + dot(scaled, win[0, pl.ds(start, 768)])
        upper = upper + dot(scaled, win[1, pl.ds(start, 768)])
        return gate, upper, square

    def arrived(o, carry):
        for dx in (0, 1, 3, 2):
            copy_e(dx, o).wait_recv()
        return first_half(o, carry)

    zero = jnp.zeros((64, 256), F32)
    carry = first_half(0, (zero, zero, jnp.zeros((64, 1), F32)))
    gate, upper, square = lax.fori_loop(1, 8, arrived, carry)
    inverse = lax.rsqrt(square * (1.0 / 6144) + EPS)
    gate = gate * inverse
    act = (gate / (1.0 + jnp.exp(-gate)) * (upper * inverse)).astype(BF16)
    loads[10].wait()

    def copy_f(o):
        t = exp_at(lax.div(o, 2), lax.rem(o, 2))
        return remote(send_f.at[t], recv_f.at[e], sf.at[o], rf.at[o], exp=t)

    def copy_n(o):
        t = exp_at(lax.div(o, 2), lax.rem(o, 2))
        return remote(send_n.at[t], recv_n.at[e], sn.at[o], rn.at[o], exp=t)

    def second_half(t):
        start = pl.multiple_of(t * 768, 768)
        return (dot(act, wout[:, pl.ds(start, 768)]) * gate_col).astype(BF16)

    def produce(n):
        o = 8 - n
        t = exp_at(lax.div(o, 2), lax.rem(o, 2))
        rows = second_half(t)
        send_f[t] = rows[16:64]
        send_n[t] = rows[0:16]
        copy_f(o).start()

    loop(1, 8, produce)
    loop(1, 8, lambda o: copy_n(o).start())
    relocate(5)
    rows = second_half(e)
    recv_f[e] = rows[16:64]
    recv_n[e] = rows[0:16]
    loop(1, 8, lambda o: copy_f(o).wait_recv())
    mixed = dot(sel_far[...], recv_f[...].reshape(384, 768))
    for dx in range(1, 4):
        send_g[dx] = mixed[32 * dx - 32 : 32 * dx].astype(BF16)

    def copy_g(dx):
        return remote(send_g.at[dx], recv_g.at[dx], sg.at[dx], rg.at[dx], ctx=ctx_at(4 - dx, 0))

    def copy_h(dz):
        return remote(send_h.at[dz], recv_h.at[dz], sh.at[dz], rh.at[dz], ctx=ctx_at(0, 8 - dz))

    loop(1, 4, lambda dx: copy_g(dx).start())
    loop(1, 8, lambda o: copy_n(o).wait_recv())
    mixed = dot(sel_near[...], recv_n[...].reshape(128, 768))
    relocate(6)
    loop(1, 4, lambda dx: copy_g(dx).wait_recv())
    summed = mixed + recv_g[1].astype(F32) + recv_g[2].astype(F32) + recv_g[3].astype(F32)
    cols = [summed[:, 128 * i : 128 * i + 128].reshape(4, 8, 128) for i in range(6)]
    evens, odds = [], []
    for p in range(3):
        one, two = cols[2 * p], cols[2 * p + 1]
        evens.append(jnp.where(sub4 < 4, one, pltpu.roll(two, 4, 1)))
        odds.append(jnp.where(sub4 < 4, pltpu.roll(one, 4, 1), two))
    pad = [jnp.zeros((4, 8, 128), F32)]
    evens, odds = jnp.concatenate(evens + pad, axis=1), jnp.concatenate(odds + pad, axis=1)
    for n in range(4):
        send_h[2 * n] = evens[n].astype(BF16)
        send_h[2 * n + 1] = odds[n].astype(BF16)
    loop(1, 8, lambda dz: copy_h(dz).start())
    relocate(7)

    loop(1, 8, lambda dz: copy_h(dz).wait_recv())
    total = hidden + evens[0, 0:24]
    for dz in range(1, 8):
        total = total + recv_h[dz].astype(F32)[0:24]
    att_s[...] = total
    for i in range(6):
        lay_ref[:, 128 * i : 128 * i + 128] = att_s[4 * i : 4 * i + 4].astype(BF16)

    own_block.wait()
    loop(1, 32, lambda o: copy_r(o, lax.div(o, 8), lax.rem(o, 8)).wait_recv())
    loop(1, 4, lambda dx: copy_a(dx).wait_send())
    loop(1, 8, lambda dz: copy_b(dz).wait_send())
    loop(1, 8, lambda dz: copy_c(dz).wait_send())
    loop(1, 4, lambda dx: copy_d(dx).wait_send())
    for dx in range(4):
        loop(1, 8, lambda o, dx=dx: copy_e(dx, o).wait_send())
    loop(1, 8, lambda o: copy_f(o).wait_send())
    loop(1, 8, lambda o: copy_n(o).wait_send())
    loop(1, 4, lambda dx: copy_g(dx).wait_send())
    loop(1, 8, lambda dz: copy_h(dz).wait_send())
    loop(1, 32, lambda o: copy_r(o, lax.div(o, 8), lax.rem(o, 8)).wait_send())


def place_blocks(idxs, layer_ref, blocks_hbm, lay_ref, fin_hbm, held, came, went):
    def load(s):
        return pltpu.make_async_copy(blocks_hbm.at[idxs[1, s]], held.at[s], came.at[s])

    def store(s):
        return pltpu.make_async_copy(held.at[s], fin_hbm.at[:, s], went.at[s])

    def start(s, carry):
        @pl.when(idxs[2, s] > 0)
        def _():
            load(s).start()

        return carry

    def clear(s, carry):
        @pl.when(idxs[2, s] == 0)
        def _():
            held[s] = jnp.zeros((2, 128, 128), BF16)
            store(s).start()

        return carry

    def forward(s, carry):
        @pl.when(idxs[2, s] > 0)
        def _():
            load(s).wait()
            store(s).start()

        return carry

    def finish(s, carry):
        store(s).wait()
        return carry

    lax.fori_loop(0, 16, start, 0)
    lay_ref[...] = layer_ref[...]
    lax.fori_loop(0, 16, clear, 0)
    lax.fori_loop(0, 16, forward, 0)
    lax.fori_loop(0, 16, finish, 0)


def per_device(
    queries, new_kv, kv_cache, residual, kept_blocks, block_moves, expert_ids, gate_weights, norm_gain, expert_in,
    expert_out,
):
    vmem = pl.BlockSpec(memory_space=pltpu.VMEM)
    hbm = pl.BlockSpec(memory_space=pl.ANY)
    dma = pltpu.SemaphoreType.DMA
    layer, blocks, index = pl.pallas_call(
        kernel,
        out_shape=(
            jax.ShapeDtypeStruct((4, 768), BF16),
            jax.ShapeDtypeStruct((32, 2, 128, 128), BF16),
            jax.ShapeDtypeStruct((8, 128), I32),
        ),
        in_specs=[hbm] * 11,
        out_specs=(vmem, hbm, vmem),
        scratch_shapes=[
            pltpu.VMEM((1, 512), I32),
            pltpu.VMEM((2, 4, 128), I32),
            pltpu.VMEM((2, 16, 128, 128), BF16),
            pltpu.VMEM((6, 128, 128), BF16),
            pltpu.VMEM((4, 2, 128), BF16),
            pltpu.VMEM((4, 768), BF16),
            pltpu.VMEM((2, 128), I32),
            pltpu.VMEM((2, 128), F32),
            pltpu.VMEM((48, 128), F32),
            pltpu.VMEM((2, 6144, 256), BF16),
            pltpu.VMEM((256, 6144), BF16),
            pltpu.SMEM((8, 128), I32),
            pltpu.VMEM((4, 8, 32, 128), BF16),
            pltpu.VMEM((4, 8, 32, 128), BF16),
            pltpu.VMEM((8, 32, 128), BF16),
            pltpu.VMEM((8, 32, 128), BF16),
            pltpu.VMEM((4, 8, 32, 128), BF16),
            pltpu.VMEM((8, 64, 768), BF16),
            pltpu.VMEM((8, 64, 768), BF16),
            pltpu.VMEM((8, 48, 768), BF16),
            pltpu.VMEM((8, 48, 768), BF16),
            pltpu.VMEM((8, 16, 768), BF16),
            pltpu.VMEM((8, 16, 768), BF16),
            pltpu.VMEM((4, 32, 768), BF16),
            pltpu.VMEM((4, 32, 768), BF16),
            pltpu.VMEM((8, 32, 128), BF16),
            pltpu.VMEM((8, 32, 128), BF16),
            pltpu.VMEM((32, 2, 128, 128), BF16),
            pltpu.VMEM((8, 128), F32),
            pltpu.VMEM((8, 128), F32),
            pltpu.VMEM((8, 128), F32),
            pltpu.VMEM((8, 128), I32),
            pltpu.VMEM((8, 128), F32),
            pltpu.VMEM((96, 384), BF16),
            pltpu.VMEM((32, 128), BF16),
            pltpu.VMEM((24, 128), F32),
            pltpu.VMEM((24, 128), F32),
            dma((13,)),
            dma((4,)), dma((4,)),
            dma((8,)), dma((8,)),
            dma((8,)), dma((8,)),
            dma((4,)), dma((4,)),
            dma((32,)), dma((32,)),
            dma((8,)), dma((8,)),
            dma((8,)), dma((8,)),
            dma((4,)), dma((4,)),
            dma((8,)), dma((8,)),
            dma((32,)), dma((32,)),
        ],
        compiler_params=pltpu.CompilerParams(
            collective_id=0, has_side_effects=True, vmem_limit_bytes=60 * 1024 * 1024
        ),
        name="layer",
    )(
        block_moves.reshape(1, 512),
        jnp.transpose(kept_blocks[:, 0], (0, 2, 1)),
        kv_cache.reshape(2, 16, 128, 128),
        jnp.transpose(queries[0], (1, 0, 2)),
        new_kv.reshape(4, 2, 128),
        residual.reshape(4, 768),
        expert_ids[0].T,
        gate_weights[0].T,
        norm_gain.reshape(48, 128),
        expert_in.reshape(2, 6144, 256),
        expert_out.reshape(256, 6144),
    )
    layer, final = pl.pallas_call(
        place_blocks,
        out_shape=(
            jax.ShapeDtypeStruct((4, 768), BF16),
            jax.ShapeDtypeStruct((2, 16, 128, 128), BF16),
        ),
        in_specs=[pl.BlockSpec(memory_space=pltpu.SMEM), vmem, hbm],
        out_specs=(vmem, hbm),
        scratch_shapes=[pltpu.VMEM((16, 2, 128, 128), BF16), dma((16,)), dma((16,))],
        compiler_params=pltpu.CompilerParams(vmem_limit_bytes=60 * 1024 * 1024),
        name="place_blocks",
    )(index, layer, blocks)
    return layer.reshape(1, 4, 768), final.reshape(2, 1, 16, 128, 128)


def solution(mesh):
    in_specs = (
        P(None, None, "exp", None),
        P(None, "ctx", None, "exp", None),
        P(None, "exp", "ctx", None, None),
        P(None, "ctx", "exp"),
        P(None, "exp", None, None),
        P(None, "exp", None),
        P(),
        P(),
        P(),
        P("exp", None, None, "ctx"),
        P("exp", "ctx", None),
    )
    out_specs = (P(None, "ctx", "exp"), P(None, "exp", "ctx", None, None))
    return jax.shard_map(
        per_device, mesh=mesh, in_specs=in_specs, out_specs=out_specs, check_vma=False
    )
```

```python
import functools
import math

import jax
import jax.numpy as jnp
from jax import lax
from jax.experimental import pallas as pl
from jax.experimental.pallas import tpu as pltpu
from jax.sharding import PartitionSpec as P

MESH = pl.DeviceIdType.MESH
NEG = -1e30
EPS = 1e-05
F32, BF16, I32 = jnp.float32, jnp.bfloat16, jnp.int32

def along_z(*dzs):
    return tuple((0, dz) for dz in dzs)


def mixed_with(*dzs):
    return tuple((dx, dz) for dz in dzs for dx in (2, 1, 3))


ALONG_X = ((2, 0), (1, 0), (3, 0))
STAGES = (
    along_z(1, 7, 2, 6),
    ALONG_X,
    along_z(3, 5, 4) + mixed_with(1),
    mixed_with(4, 3, 5),
    mixed_with(2, 6, 7),
    (),
    (),
    (),
)


def iota(shape, dim):
    return lax.broadcasted_iota(I32, shape, dim)


def dot(a, b):
    return jnp.dot(a, b, preferred_element_type=F32)


def dot_nt(a, b):
    return lax.dot_general(a, b, (((1,), (1,)), ((), ())), preferred_element_type=F32)


def split3(v):
    first = v.astype(BF16).astype(F32)
    second = (v - first).astype(BF16).astype(F32)
    return first, second, v - first - second


def kernel(
    moves_hbm, kept_hbm, cache_hbm, q_hbm, nkv_hbm, res_hbm, ids_hbm, gates_hbm, gain_hbm, win_hbm, wout_hbm,
    lay_ref, recv_r, idxv,
    moves_ref, kept_ref, cache, q_ref, nkv_ref, res_ref, ids_ref, gates_ref, gain_ref, win, wout, idxs,
    send_a, recv_a, send_b, recv_b, gx, send_e, recv_e, send_f, recv_f, send_n, recv_n, send_g, recv_g, send_h, recv_h,
    send_r, scr, nks, nvs, slots, gatev, sel_far, sel_near, att_s, res_s,
    lsem, sa, ra, sb, rb, sc, rc, sd, rd, se, re, sf, rf, sn, rn, sg, rg, sh, rh, sr, rr,
):
    c = lax.axis_index("ctx")
    e = lax.axis_index("exp")
    x, z = lax.div(c, 8), lax.rem(c, 8)
    y, k = lax.div(e, 2), lax.rem(e, 2)
    scale = 1.0 / math.sqrt(128)

    def ctx_at(dx, dz):
        return lax.rem(x + dx, 4) * 8 + lax.rem(z + dz, 8)

    def exp_at(dy, dk):
        return lax.rem(y + dy, 4) * 2 + lax.rem(k + dk, 2)

    def remote(src, dst, s, r, ctx=None, exp=None):
        return pltpu.make_async_remote_copy(
            src_ref=src, dst_ref=dst, send_sem=s, recv_sem=r,
            device_id=(c if ctx is None else ctx, e if exp is None else exp), device_id_type=MESH,
        )

    sources = (moves_hbm, kept_hbm, cache_hbm, q_hbm, nkv_hbm, res_hbm, ids_hbm, gates_hbm, gain_hbm, win_hbm, wout_hbm)
    targets = (moves_ref, kept_ref, cache, q_ref, nkv_ref, res_ref, ids_ref, gates_ref, gain_ref, win, wout)
    loads = [pltpu.make_async_copy(a, b, lsem.at[i]) for i, (a, b) in enumerate(zip(sources, targets))]
    for load in loads[:9]:
        load.start()

    barrier = pltpu.get_barrier_semaphore()

    def greet_ctx(o, carry):
        pl.semaphore_signal(
            barrier, inc=1, device_id=(ctx_at(lax.div(o, 8), lax.rem(o, 8)), e), device_id_type=MESH
        )
        return carry

    def greet_exp(o, carry):
        pl.semaphore_signal(
            barrier, inc=1, device_id=(c, exp_at(lax.div(o, 2), lax.rem(o, 2))), device_id_type=MESH
        )
        return carry

    lax.fori_loop(1, 32, greet_ctx, 0)
    lax.fori_loop(1, 8, greet_exp, 0)

    loads[0].wait()
    loads[1].wait()
    mv = moves_ref[...]
    lane = iota((32, 512), 1)
    off = iota((32, 512), 0)
    target = ((x + (off >> 3)) & 3) * 8 + ((z + (off & 7)) & 7)
    hit = ((mv >> 4) == target) & ((lane >> 4) == c)
    srcj = jnp.max(jnp.where(hit, lane & 15, 0), axis=1, keepdims=True)
    lane = iota((16, 512), 1)
    hit = mv == 16 * c + iota((16, 512), 0)
    place = ((x - (lane >> 7)) & 3) * 8 + ((z - ((lane >> 4) & 7)) & 7)
    rslot = jnp.max(jnp.where(hit, place, 0), axis=1, keepdims=True)
    kept1 = kept_ref[1]
    slot16 = 16 * c + iota((16, 128), 0)
    alive = kept1[0:1] == slot16
    for j in range(1, 4):
        alive = alive | (kept1[j : j + 1] == slot16)
    living = jnp.max(jnp.where(alive, 1, 0), axis=1, keepdims=True)
    eye32 = iota((32, 128), 0) == iota((32, 128), 1)
    eye16 = iota((16, 128), 0) == iota((16, 128), 1)
    idxv[0:1, :] = jnp.sum(jnp.where(eye32, srcj, 0), axis=0, keepdims=True)
    idxv[1:2, :] = jnp.sum(jnp.where(eye16, rslot, 0), axis=0, keepdims=True)
    idxv[2:3, :] = jnp.sum(jnp.where(eye16, living, 0), axis=0, keepdims=True)
    to_smem = pltpu.make_async_copy(idxv, idxs, lsem.at[11])
    to_smem.start()

    def copy_a(dx):
        row = lax.rem(x + dx, 4)
        return remote(send_a.at[row], recv_a.at[dx], sa.at[dx], ra.at[dx], ctx=row * 8 + z)

    def copy_b(dz):
        to = lax.rem(z + dz, 8)
        return remote(send_b.at[to], recv_b.at[dz], sb.at[dz], rb.at[dz], ctx=x * 8 + to)

    def copy_r(o, dx, dz):
        return remote(send_r.at[o], recv_r.at[o], sr.at[o], rr.at[o], ctx=ctx_at(dx, dz))

    def relocate(stage):
        for dx, dz in STAGES[stage]:
            copy_r(dx * 8 + dz, dx, dz).start()

    def loop(lo, hi, body):
        def step(o, carry):
            body(o)
            return carry

        lax.fori_loop(lo, hi, step, 0)

    rsub, rlane = iota((128, 128), 0), iota((128, 128), 1)
    kept0 = kept_ref[0]
    slot_id = 16 * c + (rsub & 15)
    owned = kept0[0:1] == slot_id
    for j in range(1, 4):
        owned = owned | (kept0[j : j + 1] == slot_id)
    owned = owned & (rsub < 96)
    ownf = jnp.where(owned, 1.0, 0.0)
    ownb = ownf.astype(BF16)
    owncol = jnp.sum(jnp.where(owned, rlane, 0), axis=1, keepdims=True)
    ownrow = dot_nt(iota((8, 128), 1).astype(F32).astype(BF16), ownb)[0:1].astype(I32)
    loads[3].wait()
    heads = [dot(ownb[16 * i : 16 * i + 16], q_ref[i]) for i in range(6)]
    q96 = jnp.concatenate(heads + [jnp.zeros((32, 128), F32)], axis=0).astype(BF16)
    loads[2].wait()
    loads[9].start()
    loads[10].start()
    scores = jnp.zeros((128, 128), F32)
    for j in range(16):
        scores = jnp.where((rsub & 15) == j, dot_nt(q96, cache[0, j]), scores)
    scores = scores * scale
    m = jnp.max(scores, axis=1, keepdims=True)
    probs = jnp.exp(scores - m).astype(BF16)
    l = jnp.sum(probs.astype(F32), axis=1, keepdims=True)
    out = jnp.zeros((128, 128), F32)
    for j in range(16):
        out = jnp.where((rsub & 15) == j, dot(probs, cache[1, j]), out)
    eye = rsub == rlane
    same = (owncol == ownrow) & ((rsub >> 4) == (rlane >> 4))
    mrow = jnp.sum(jnp.where(eye, m, 0.0), axis=0, keepdims=True)
    mseq = jnp.max(jnp.where(same, mrow, NEG), axis=1, keepdims=True)
    f = jnp.exp(m - mseq)
    lrow = jnp.sum(jnp.where(eye, l * f, 0.0), axis=0, keepdims=True)
    lseq = jnp.sum(jnp.where(same, lrow, 0.0), axis=1, keepdims=True)
    first = jnp.min(jnp.where(same, rlane.astype(F32), 999.0), axis=1, keepdims=True)
    place = ((rsub >> 4) << 2) + (owncol & 3)
    spread = (place == rlane) & (first == rsub.astype(F32)) & (rsub < 96)
    stats = [jnp.where(spread, v, 0.0).astype(BF16) for v in split3(mseq) + split3(lseq)]
    rl = iota((1, 128), 1)
    code = jnp.where(rl < 96, ((ownrow >> 2) << 5) + ((rl >> 4) << 2) + (ownrow & 3), -1)
    lift = jnp.where(iota((1024, 128), 0) == code, 1.0, 0.0).astype(BF16)
    values = dot(lift, (out * f).astype(BF16)).reshape(32, 32, 128)
    code = jnp.where(rl < 96, (ownrow >> 2) << 3, -100)
    row256 = iota((256, 128), 0)
    lift = jnp.concatenate([jnp.where(row256 == code + t, 1.0, 0.0).astype(BF16) for t in range(6)], axis=1)
    stat = dot(lift, jnp.concatenate(stats, axis=0)).reshape(32, 8, 128)
    send_a[...] = jnp.concatenate([values[:, 0:24], stat], axis=1).astype(BF16).reshape(4, 8, 32, 128)

    pl.semaphore_wait(barrier, 38)
    loop(1, 4, lambda dx: copy_a(dx).start())
    recv_a[0] = send_a[x]

    to_smem.wait()

    def pack(o, carry):
        send_r[o] = cache[:, idxs[0, o]]
        return carry

    lax.fori_loop(0, 32, pack, 0)

    relocate(0)
    own_block = pltpu.make_async_copy(send_r.at[0], recv_r.at[0], lsem.at[12])
    own_block.start()

    for load in loads[4:9]:
        load.wait()
    res = res_ref[...].astype(F32)
    nks[0:4] = nkv_ref[:, 0].astype(F32)
    nks[4:8] = nkv_ref[:, 0].astype(F32)
    nvs[0:4] = nkv_ref[:, 1].astype(F32)
    nvs[4:8] = nkv_ref[:, 1].astype(F32)
    for i in range(6):
        res_s[4 * i : 4 * i + 4] = res[:, 128 * i : 128 * i + 128]
    s8, b8 = iota((8, 128), 0), iota((8, 128), 1)
    low = jnp.where((s8 < 4) & (b8 == 4 * c + s8), 1.0, 0.0).astype(BF16)
    high = jnp.where((s8 >= 4) & (b8 == 4 * c + s8 - 4), 1.0, 0.0).astype(BF16)
    q24 = jnp.concatenate([dot(low, q_ref[2 * p]) + dot(high, q_ref[2 * p + 1]) for p in range(3)], axis=0)
    nk24 = jnp.concatenate([nks[...]] * 3, axis=0)
    nv24 = jnp.concatenate([nvs[...]] * 3, axis=0)
    own_score = jnp.sum(q24 * nk24, axis=1, keepdims=True) * scale
    eye24 = iota((24, 128), 0) == iota((24, 128), 1)
    own_score = jnp.sum(jnp.where(eye24, own_score, 0.0), axis=0, keepdims=True)

    g3 = split3(gates_ref[...])
    scr[0:2] = ids_ref[...].astype(F32)
    for i in range(3):
        scr[2 * i + 2 : 2 * i + 4] = g3[i]
    o128 = rlane >> 2
    group = ((x - (o128 >> 3)) & 3) * 8 + ((z - (o128 & 7)) & 7)
    relative = jnp.where(rsub == 4 * group + (rlane & 3), 1.0, 0.0).astype(BF16)
    routed = dot(scr[...].astype(BF16), relative)
    r0, r1 = routed[0:1].astype(I32), routed[1:2].astype(I32)
    w0 = routed[2:3] + routed[4:5] + routed[6:7]
    w1 = routed[3:4] + routed[5:6] + routed[7:8]
    goes = jnp.where((r0 == s8) | (r1 == s8), 1, 0)
    rank = jnp.zeros((8, 128), I32)
    for d in range(1, 4):
        rank = rank + jnp.where((b8 & 3) >= d, pltpu.roll(goes, d, 1), 0)
    slot = jnp.where(goes > 0, ((b8 >> 2) << 1) + rank, -1)
    slots[...] = slot
    gatev[...] = jnp.where(r0 == s8, w0, 0.0) + jnp.where(r1 == s8, w1, 0.0)
    row64 = iota((64, 128), 0)
    sel = jnp.concatenate([jnp.where(row64 == slot[j : j + 1], 1.0, 0.0) for j in range(8)], axis=0)
    picks = []
    for dx in range(4):
        block = jnp.concatenate([sel[64 * j + 16 * dx : 64 * j + 16 * dx + 16] for j in range(8)], axis=0)
        if dx:
            block = pltpu.roll(block, 128 - 32 * dx, 1)
        picks.append(block[:, 0:32].astype(BF16))
    far_rows = jnp.concatenate([sel[64 * j + 16 : 64 * j + 64] for j in range(8)], axis=0).T
    near_rows = jnp.concatenate([sel[64 * j : 64 * j + 16] for j in range(8)], axis=0).T
    sel_far[...] = far_rows[32:128].astype(BF16)
    sel_near[...] = near_rows[0:32].astype(BF16)
    gate_col = jnp.sum(
        jnp.where(row64 == slots[pl.ds(e, 1)], gatev[pl.ds(e, 1)], 0.0), axis=1, keepdims=True
    )

    def unpack(got):
        st = got[:, 24:32]
        qi = iota(st.shape, 1)
        m = jnp.sum(jnp.where(qi < 3, st, 0.0), axis=1, keepdims=True)
        l = jnp.sum(jnp.where((qi >= 3) & (qi < 6), st, 0.0), axis=1, keepdims=True)
        return jnp.where(l > 0, m, NEG), l

    def column(w):
        wide = jnp.broadcast_to(w, (w.shape[0], 24, 128))
        return jnp.sum(jnp.where(eye24[None], wide, 0.0), axis=2, keepdims=True)

    loop(1, 4, lambda dx: copy_a(dx).wait_recv())
    got = recv_a[...].astype(F32).reshape(32, 32, 128)
    m, l = unpack(got)
    m, l = m.reshape(4, 8, 1, 128), l.reshape(4, 8, 1, 128)
    top = jnp.max(m, axis=0)
    w = jnp.where(l > 0, jnp.exp(m - top[None]), 0.0)
    l = jnp.sum(w * l, axis=0)
    parts = split3(jnp.where(l > 0, top, 0.0)) + split3(l)
    qi = iota((8, 8, 128), 1)
    stat = jnp.zeros((8, 8, 128), F32)
    for n in range(6):
        stat = jnp.where(qi == n, parts[n], stat)
    values = column(w.reshape(32, 1, 128)) * got[:, 0:24]
    values = jnp.sum(values.reshape(4, 8, 24, 128), axis=0)
    send_b[...] = jnp.concatenate([values, stat], axis=1).astype(BF16)
    loop(1, 8, lambda dz: copy_b(dz).start())
    recv_b[0] = send_b[z]
    relocate(1)
    loop(1, 8, lambda dz: copy_b(dz).wait_recv())
    got = recv_b[...].astype(F32)
    m, l = unpack(got)
    top = jnp.maximum(jnp.max(m, axis=0), own_score)
    w = jnp.where(l > 0, jnp.exp(m - top[None]), 0.0)
    fresh = jnp.exp(own_score - top)
    inv_den = 1.0 / (jnp.sum(w * l, axis=0) + fresh)
    att = jnp.sum(column(w * inv_den[None]) * got[:, 0:24], axis=0)
    fcol = jnp.sum(jnp.where(eye24, fresh * inv_den, 0.0), axis=1, keepdims=True)
    att = att + fcol * nv24
    hidden = (res_s[...] + att).astype(BF16).astype(F32)
    gx[0, 0] = jnp.concatenate([hidden, jnp.zeros((8, 128), F32)], axis=0).astype(BF16)

    def copy_c(dz):
        return remote(gx.at[0, 0], gx.at[0, dz], sc.at[dz], rc.at[dz], ctx=ctx_at(0, dz))

    def copy_d(dx):
        return remote(gx.at[0], gx.at[dx], sd.at[dx], rd.at[dx], ctx=ctx_at(dx, 0))

    def copy_e(dx, o):
        t = exp_at(lax.div(o, 2), lax.rem(o, 2))
        rows = pl.ds(16 * dx, 16)
        return remote(send_e.at[t, rows], recv_e.at[e, rows], se.at[8 * dx + o], re.at[8 * dx + o], exp=t)

    def dispatch(dx):
        flat = gx[dx].astype(F32).reshape(4, 2, 32, 128)
        parts = []
        for p in range(3):
            one, two = flat[:, 0, 8 * p : 8 * p + 8], flat[:, 1, 8 * p : 8 * p + 8]
            parts.append(jnp.where(sub4 < 4, one, pltpu.roll(two, 4, 1)).reshape(32, 128).astype(BF16))
            parts.append(jnp.where(sub4 < 4, pltpu.roll(one, 4, 1), two).reshape(32, 128).astype(BF16))
        rows = dot(picks[dx], jnp.concatenate(parts, axis=1)).astype(BF16)
        for j in range(8):
            send_e[j, 16 * dx : 16 * dx + 16] = rows[16 * j : 16 * j + 16]
        loop(1, 8, lambda o: copy_e(dx, o).start())

    sub4 = iota((4, 8, 128), 1)
    loop(1, 8, lambda dz: copy_c(dz).start())
    relocate(2)
    loop(1, 8, lambda dz: copy_c(dz).wait_recv())
    loop(1, 4, lambda dx: copy_d(dx).start())
    dispatch(0)
    relocate(3)
    for dx in (1, 3, 2):
        copy_d(dx).wait_recv()
        dispatch(dx)
    relocate(4)
    recv_e[e] = send_e[e]
    loads[9].wait()

    def first_half(o, carry):
        gate, upper, square = carry
        src = lax.rem(y + 4 - lax.div(o, 2), 4) * 2 + lax.rem(k + lax.rem(o, 2), 2)
        rows = recv_e[src].astype(F32)
        square = square + jnp.sum(rows * rows, axis=1, keepdims=True)
        gain = jnp.concatenate([gain_ref[pl.ds(6 * src + i, 1)] for i in range(6)], axis=1)
        scaled = (rows * gain).astype(BF16)
        start = pl.multiple_of(src * 768, 768)
        gate = gate + dot(scaled, win[0, pl.ds(start, 768)])
        upper = upper + dot(scaled, win[1, pl.ds(start, 768)])
        return gate, upper, square

    def arrived(o, carry):
        for dx in (0, 1, 3, 2):
            copy_e(dx, o).wait_recv()
        return first_half(o, carry)

    zero = jnp.zeros((64, 256), F32)
    carry = first_half(0, (zero, zero, jnp.zeros((64, 1), F32)))
    gate, upper, square = lax.fori_loop(1, 8, arrived, carry)
    inverse = lax.rsqrt(square * (1.0 / 6144) + EPS)
    gate = gate * inverse
    act = (gate / (1.0 + jnp.exp(-gate)) * (upper * inverse)).astype(BF16)
    loads[10].wait()

    def copy_f(o):
        t = exp_at(lax.div(o, 2), lax.rem(o, 2))
        return remote(send_f.at[t], recv_f.at[e], sf.at[o], rf.at[o], exp=t)

    def copy_n(o):
        t = exp_at(lax.div(o, 2), lax.rem(o, 2))
        return remote(send_n.at[t], recv_n.at[e], sn.at[o], rn.at[o], exp=t)

    def second_half(t):
        start = pl.multiple_of(t * 768, 768)
        return (dot(act, wout[:, pl.ds(start, 768)]) * gate_col).astype(BF16)

    def produce(n):
        o = 8 - n
        t = exp_at(lax.div(o, 2), lax.rem(o, 2))
        rows = second_half(t)
        send_f[t] = rows[16:64]
        send_n[t] = rows[0:16]
        copy_f(o).start()

    loop(1, 8, produce)
    loop(1, 8, lambda o: copy_n(o).start())
    relocate(5)
    rows = second_half(e)
    recv_f[e] = rows[16:64]
    recv_n[e] = rows[0:16]
    loop(1, 8, lambda o: copy_f(o).wait_recv())
    mixed = dot(sel_far[...], recv_f[...].reshape(384, 768))
    for dx in range(1, 4):
        send_g[dx] = mixed[32 * dx - 32 : 32 * dx].astype(BF16)

    def copy_g(dx):
        return remote(send_g.at[dx], recv_g.at[dx], sg.at[dx], rg.at[dx], ctx=ctx_at(4 - dx, 0))

    def copy_h(dz):
        return remote(send_h.at[dz], recv_h.at[dz], sh.at[dz], rh.at[dz], ctx=ctx_at(0, 8 - dz))

    loop(1, 4, lambda dx: copy_g(dx).start())
    loop(1, 8, lambda o: copy_n(o).wait_recv())
    mixed = dot(sel_near[...], recv_n[...].reshape(128, 768))
    relocate(6)
    loop(1, 4, lambda dx: copy_g(dx).wait_recv())
    summed = mixed + recv_g[1].astype(F32) + recv_g[2].astype(F32) + recv_g[3].astype(F32)
    cols = [summed[:, 128 * i : 128 * i + 128].reshape(4, 8, 128) for i in range(6)]
    evens, odds = [], []
    for p in range(3):
        one, two = cols[2 * p], cols[2 * p + 1]
        evens.append(jnp.where(sub4 < 4, one, pltpu.roll(two, 4, 1)))
        odds.append(jnp.where(sub4 < 4, pltpu.roll(one, 4, 1), two))
    pad = [jnp.zeros((4, 8, 128), F32)]
    evens, odds = jnp.concatenate(evens + pad, axis=1), jnp.concatenate(odds + pad, axis=1)
    for n in range(4):
        send_h[2 * n] = evens[n].astype(BF16)
        send_h[2 * n + 1] = odds[n].astype(BF16)
    loop(1, 8, lambda dz: copy_h(dz).start())
    relocate(7)

    loop(1, 8, lambda dz: copy_h(dz).wait_recv())
    total = hidden + evens[0, 0:24]
    for dz in range(1, 8):
        total = total + recv_h[dz].astype(F32)[0:24]
    att_s[...] = total
    for i in range(6):
        lay_ref[:, 128 * i : 128 * i + 128] = att_s[4 * i : 4 * i + 4].astype(BF16)

    own_block.wait()
    loop(1, 32, lambda o: copy_r(o, lax.div(o, 8), lax.rem(o, 8)).wait_recv())
    loop(1, 4, lambda dx: copy_a(dx).wait_send())
    loop(1, 8, lambda dz: copy_b(dz).wait_send())
    loop(1, 8, lambda dz: copy_c(dz).wait_send())
    loop(1, 4, lambda dx: copy_d(dx).wait_send())
    for dx in range(4):
        loop(1, 8, lambda o, dx=dx: copy_e(dx, o).wait_send())
    loop(1, 8, lambda o: copy_f(o).wait_send())
    loop(1, 8, lambda o: copy_n(o).wait_send())
    loop(1, 4, lambda dx: copy_g(dx).wait_send())
    loop(1, 8, lambda dz: copy_h(dz).wait_send())
    loop(1, 32, lambda o: copy_r(o, lax.div(o, 8), lax.rem(o, 8)).wait_send())


def place_blocks(idxs, layer_ref, blocks_hbm, lay_ref, fin_hbm, held, came, went):
    def load(s):
        return pltpu.make_async_copy(blocks_hbm.at[idxs[1, s]], held.at[s], came.at[s])

    def store(s):
        return pltpu.make_async_copy(held.at[s], fin_hbm.at[:, s], went.at[s])

    def start(s, carry):
        @pl.when(idxs[2, s] > 0)
        def _():
            load(s).start()

        return carry

    def clear(s, carry):
        @pl.when(idxs[2, s] == 0)
        def _():
            held[s] = jnp.zeros((2, 128, 128), BF16)
            store(s).start()

        return carry

    def forward(s, carry):
        @pl.when(idxs[2, s] > 0)
        def _():
            load(s).wait()
            store(s).start()

        return carry

    def finish(s, carry):
        store(s).wait()
        return carry

    lax.fori_loop(0, 16, start, 0)
    lay_ref[...] = layer_ref[...]
    lax.fori_loop(0, 16, clear, 0)
    lax.fori_loop(0, 16, forward, 0)
    lax.fori_loop(0, 16, finish, 0)


def per_device(
    queries, new_kv, kv_cache, residual, kept_blocks, block_moves, expert_ids, gate_weights, norm_gain, expert_in,
    expert_out,
):
    vmem = pl.BlockSpec(memory_space=pltpu.VMEM)
    hbm = pl.BlockSpec(memory_space=pl.ANY)
    dma = pltpu.SemaphoreType.DMA
    layer, blocks, index = pl.pallas_call(
        kernel,
        out_shape=(
            jax.ShapeDtypeStruct((4, 768), BF16),
            jax.ShapeDtypeStruct((32, 2, 128, 128), BF16),
            jax.ShapeDtypeStruct((8, 128), I32),
        ),
        in_specs=[hbm] * 11,
        out_specs=(vmem, hbm, vmem),
        scratch_shapes=[
            pltpu.VMEM((1, 512), I32),
            pltpu.VMEM((2, 4, 128), I32),
            pltpu.VMEM((2, 16, 128, 128), BF16),
            pltpu.VMEM((6, 128, 128), BF16),
            pltpu.VMEM((4, 2, 128), BF16),
            pltpu.VMEM((4, 768), BF16),
            pltpu.VMEM((2, 128), I32),
            pltpu.VMEM((2, 128), F32),
            pltpu.VMEM((48, 128), F32),
            pltpu.VMEM((2, 6144, 256), BF16),
            pltpu.VMEM((256, 6144), BF16),
            pltpu.SMEM((8, 128), I32),
            pltpu.VMEM((4, 8, 32, 128), BF16),
            pltpu.VMEM((4, 8, 32, 128), BF16),
            pltpu.VMEM((8, 32, 128), BF16),
            pltpu.VMEM((8, 32, 128), BF16),
            pltpu.VMEM((4, 8, 32, 128), BF16),
            pltpu.VMEM((8, 64, 768), BF16),
            pltpu.VMEM((8, 64, 768), BF16),
            pltpu.VMEM((8, 48, 768), BF16),
            pltpu.VMEM((8, 48, 768), BF16),
            pltpu.VMEM((8, 16, 768), BF16),
            pltpu.VMEM((8, 16, 768), BF16),
            pltpu.VMEM((4, 32, 768), BF16),
            pltpu.VMEM((4, 32, 768), BF16),
            pltpu.VMEM((8, 32, 128), BF16),
            pltpu.VMEM((8, 32, 128), BF16),
            pltpu.VMEM((32, 2, 128, 128), BF16),
            pltpu.VMEM((8, 128), F32),
            pltpu.VMEM((8, 128), F32),
            pltpu.VMEM((8, 128), F32),
            pltpu.VMEM((8, 128), I32),
            pltpu.VMEM((8, 128), F32),
            pltpu.VMEM((96, 384), BF16),
            pltpu.VMEM((32, 128), BF16),
            pltpu.VMEM((24, 128), F32),
            pltpu.VMEM((24, 128), F32),
            dma((13,)),
            dma((4,)), dma((4,)),
            dma((8,)), dma((8,)),
            dma((8,)), dma((8,)),
            dma((4,)), dma((4,)),
            dma((32,)), dma((32,)),
            dma((8,)), dma((8,)),
            dma((8,)), dma((8,)),
            dma((4,)), dma((4,)),
            dma((8,)), dma((8,)),
            dma((32,)), dma((32,)),
        ],
        compiler_params=pltpu.CompilerParams(
            collective_id=0, has_side_effects=True, vmem_limit_bytes=60 * 1024 * 1024
        ),
        name="layer",
    )(
        block_moves.reshape(1, 512),
        jnp.transpose(kept_blocks[:, 0], (0, 2, 1)),
        kv_cache.reshape(2, 16, 128, 128),
        jnp.transpose(queries[0], (1, 0, 2)),
        new_kv.reshape(4, 2, 128),
        residual.reshape(4, 768),
        expert_ids[0].T,
        gate_weights[0].T,
        norm_gain.reshape(48, 128),
        expert_in.reshape(2, 6144, 256),
        expert_out.reshape(256, 6144),
    )
    layer, final = pl.pallas_call(
        place_blocks,
        out_shape=(
            jax.ShapeDtypeStruct((4, 768), BF16),
            jax.ShapeDtypeStruct((2, 16, 128, 128), BF16),
        ),
        in_specs=[pl.BlockSpec(memory_space=pltpu.SMEM), vmem, hbm],
        out_specs=(vmem, hbm),
        scratch_shapes=[pltpu.VMEM((16, 2, 128, 128), BF16), dma((16,)), dma((16,))],
        compiler_params=pltpu.CompilerParams(vmem_limit_bytes=60 * 1024 * 1024),
        name="place_blocks",
    )(index, layer, blocks)
    return layer.reshape(1, 4, 768), final.reshape(2, 1, 16, 128, 128)


def solution(mesh):
    in_specs = (
        P(None, None, "exp", None),
        P(None, "ctx", None, "exp", None),
        P(None, "exp", "ctx", None, None),
        P(None, "ctx", "exp"),
        P(None, "exp", None, None),
        P(None, "exp", None),
        P(),
        P(),
        P(),
        P("exp", None, None, "ctx"),
        P("exp", "ctx", None),
    )
    out_specs = (P(None, "ctx", "exp"), P(None, "exp", "ctx", None, None))
    return jax.shard_map(
        per_device, mesh=mesh, in_specs=in_specs, out_specs=out_specs, check_vma=False
    )
```

```python
import functools
import math

import jax
import jax.numpy as jnp
from jax import lax
from jax.experimental import pallas as pl
from jax.experimental.pallas import tpu as pltpu
from jax.sharding import PartitionSpec as P

MESH = pl.DeviceIdType.MESH
NEG = -1e30
EPS = 1e-05
F32, BF16, I32 = jnp.float32, jnp.bfloat16, jnp.int32

def along_z(*dzs):
    return tuple((0, dz) for dz in dzs)


def mixed_with(*dzs):
    return tuple((dx, dz) for dz in dzs for dx in (2, 1, 3))


ALONG_X = ((2, 0), (1, 0), (3, 0))
STAGES = (
    along_z(1, 7, 2, 6),
    ALONG_X,
    along_z(3, 5, 4) + mixed_with(1, 7),
    mixed_with(4, 3, 5),
    mixed_with(2, 6),
    (),
    (),
    (),
)


def iota(shape, dim):
    return lax.broadcasted_iota(I32, shape, dim)


def dot(a, b):
    return jnp.dot(a, b, preferred_element_type=F32)


def dot_nt(a, b):
    return lax.dot_general(a, b, (((1,), (1,)), ((), ())), preferred_element_type=F32)


def split3(v):
    first = v.astype(BF16).astype(F32)
    second = (v - first).astype(BF16).astype(F32)
    return first, second, v - first - second


def kernel(
    moves_hbm, kept_hbm, cache_hbm, q_hbm, nkv_hbm, res_hbm, ids_hbm, gates_hbm, gain_hbm, win_hbm, wout_hbm,
    lay_ref, recv_r, idxv,
    moves_ref, kept_ref, cache, q_ref, nkv_ref, res_ref, ids_ref, gates_ref, gain_ref, win, wout, idxs,
    send_a, recv_a, send_b, recv_b, gx, send_e, recv_e, send_f, recv_f, send_n, recv_n, send_g, recv_g, send_h, recv_h,
    send_r, scr, nks, nvs, slots, gatev, sel_far, sel_near, att_s, res_s,
    lsem, sa, ra, sb, rb, sc, rc, sd, rd, se, re, sf, rf, sn, rn, sg, rg, sh, rh, sr, rr,
):
    c = lax.axis_index("ctx")
    e = lax.axis_index("exp")
    x, z = lax.div(c, 8), lax.rem(c, 8)
    y, k = lax.div(e, 2), lax.rem(e, 2)
    scale = 1.0 / math.sqrt(128)

    def ctx_at(dx, dz):
        return lax.rem(x + dx, 4) * 8 + lax.rem(z + dz, 8)

    def exp_at(dy, dk):
        return lax.rem(y + dy, 4) * 2 + lax.rem(k + dk, 2)

    def remote(src, dst, s, r, ctx=None, exp=None):
        return pltpu.make_async_remote_copy(
            src_ref=src, dst_ref=dst, send_sem=s, recv_sem=r,
            device_id=(c if ctx is None else ctx, e if exp is None else exp), device_id_type=MESH,
        )

    sources = (moves_hbm, kept_hbm, cache_hbm, q_hbm, nkv_hbm, res_hbm, ids_hbm, gates_hbm, gain_hbm, win_hbm, wout_hbm)
    targets = (moves_ref, kept_ref, cache, q_ref, nkv_ref, res_ref, ids_ref, gates_ref, gain_ref, win, wout)
    loads = [pltpu.make_async_copy(a, b, lsem.at[i]) for i, (a, b) in enumerate(zip(sources, targets))]
    for load in loads[:9]:
        load.start()

    barrier = pltpu.get_barrier_semaphore()

    def greet_ctx(o, carry):
        pl.semaphore_signal(
            barrier, inc=1, device_id=(ctx_at(lax.div(o, 8), lax.rem(o, 8)), e), device_id_type=MESH
        )
        return carry

    def greet_exp(o, carry):
        pl.semaphore_signal(
            barrier, inc=1, device_id=(c, exp_at(lax.div(o, 2), lax.rem(o, 2))), device_id_type=MESH
        )
        return carry

    lax.fori_loop(1, 32, greet_ctx, 0)
    lax.fori_loop(1, 8, greet_exp, 0)

    loads[0].wait()
    loads[1].wait()
    mv = moves_ref[...]
    lane = iota((32, 512), 1)
    off = iota((32, 512), 0)
    target = ((x + (off >> 3)) & 3) * 8 + ((z + (off & 7)) & 7)
    hit = ((mv >> 4) == target) & ((lane >> 4) == c)
    srcj = jnp.max(jnp.where(hit, lane & 15, 0), axis=1, keepdims=True)
    lane = iota((16, 512), 1)
    hit = mv == 16 * c + iota((16, 512), 0)
    place = ((x - (lane >> 7)) & 3) * 8 + ((z - ((lane >> 4) & 7)) & 7)
    rslot = jnp.max(jnp.where(hit, place, 0), axis=1, keepdims=True)
    kept1 = kept_ref[1]
    slot16 = 16 * c + iota((16, 128), 0)
    alive = kept1[0:1] == slot16
    for j in range(1, 4):
        alive = alive | (kept1[j : j + 1] == slot16)
    living = jnp.max(jnp.where(alive, 1, 0), axis=1, keepdims=True)
    eye32 = iota((32, 128), 0) == iota((32, 128), 1)
    eye16 = iota((16, 128), 0) == iota((16, 128), 1)
    idxv[0:1, :] = jnp.sum(jnp.where(eye32, srcj, 0), axis=0, keepdims=True)
    idxv[1:2, :] = jnp.sum(jnp.where(eye16, rslot, 0), axis=0, keepdims=True)
    idxv[2:3, :] = jnp.sum(jnp.where(eye16, living, 0), axis=0, keepdims=True)
    to_smem = pltpu.make_async_copy(idxv, idxs, lsem.at[11])
    to_smem.start()

    def copy_a(dx):
        row = lax.rem(x + dx, 4)
        return remote(send_a.at[row], recv_a.at[dx], sa.at[dx], ra.at[dx], ctx=row * 8 + z)

    def copy_b(dz):
        to = lax.rem(z + dz, 8)
        return remote(send_b.at[to], recv_b.at[dz], sb.at[dz], rb.at[dz], ctx=x * 8 + to)

    def copy_r(o, dx, dz):
        return remote(send_r.at[o], recv_r.at[o], sr.at[o], rr.at[o], ctx=ctx_at(dx, dz))

    def relocate(stage):
        for dx, dz in STAGES[stage]:
            copy_r(dx * 8 + dz, dx, dz).start()

    def loop(lo, hi, body):
        def step(o, carry):
            body(o)
            return carry

        lax.fori_loop(lo, hi, step, 0)

    rsub, rlane = iota((128, 128), 0), iota((128, 128), 1)
    kept0 = kept_ref[0]
    slot_id = 16 * c + (rsub & 15)
    owned = kept0[0:1] == slot_id
    for j in range(1, 4):
        owned = owned | (kept0[j : j + 1] == slot_id)
    owned = owned & (rsub < 96)
    ownf = jnp.where(owned, 1.0, 0.0)
    ownb = ownf.astype(BF16)
    owncol = jnp.sum(jnp.where(owned, rlane, 0), axis=1, keepdims=True)
    ownrow = dot_nt(iota((8, 128), 1).astype(F32).astype(BF16), ownb)[0:1].astype(I32)
    loads[3].wait()
    heads = [dot(ownb[16 * i : 16 * i + 16], q_ref[i]) for i in range(6)]
    q96 = jnp.concatenate(heads + [jnp.zeros((32, 128), F32)], axis=0).astype(BF16)
    loads[2].wait()
    loads[9].start()
    loads[10].start()
    scores = jnp.zeros((128, 128), F32)
    for j in range(16):
        scores = jnp.where((rsub & 15) == j, dot_nt(q96, cache[0, j]), scores)
    scores = scores * scale
    m = jnp.max(scores, axis=1, keepdims=True)
    probs = jnp.exp(scores - m).astype(BF16)
    l = jnp.sum(probs.astype(F32), axis=1, keepdims=True)
    out = jnp.zeros((128, 128), F32)
    for j in range(16):
        out = jnp.where((rsub & 15) == j, dot(probs, cache[1, j]), out)
    eye = rsub == rlane
    same = (owncol == ownrow) & ((rsub >> 4) == (rlane >> 4))
    mrow = jnp.sum(jnp.where(eye, m, 0.0), axis=0, keepdims=True)
    mseq = jnp.max(jnp.where(same, mrow, NEG), axis=1, keepdims=True)
    f = jnp.exp(m - mseq)
    lrow = jnp.sum(jnp.where(eye, l * f, 0.0), axis=0, keepdims=True)
    lseq = jnp.sum(jnp.where(same, lrow, 0.0), axis=1, keepdims=True)
    first = jnp.min(jnp.where(same, rlane.astype(F32), 999.0), axis=1, keepdims=True)
    place = ((rsub >> 4) << 2) + (owncol & 3)
    spread = (place == rlane) & (first == rsub.astype(F32)) & (rsub < 96)
    stats = [jnp.where(spread, v, 0.0).astype(BF16) for v in split3(mseq) + split3(lseq)]
    rl = iota((1, 128), 1)
    code = jnp.where(rl < 96, ((ownrow >> 2) << 5) + ((rl >> 4) << 2) + (ownrow & 3), -1)
    lift = jnp.where(iota((1024, 128), 0) == code, 1.0, 0.0).astype(BF16)
    values = dot(lift, (out * f).astype(BF16)).reshape(32, 32, 128)
    code = jnp.where(rl < 96, (ownrow >> 2) << 3, -100)
    row256 = iota((256, 128), 0)
    lift = jnp.concatenate([jnp.where(row256 == code + t, 1.0, 0.0).astype(BF16) for t in range(6)], axis=1)
    stat = dot(lift, jnp.concatenate(stats, axis=0)).reshape(32, 8, 128)
    send_a[...] = jnp.concatenate([values[:, 0:24], stat], axis=1).astype(BF16).reshape(4, 8, 32, 128)

    pl.semaphore_wait(barrier, 38)
    loop(1, 4, lambda dx: copy_a(dx).start())
    recv_a[0] = send_a[x]

    to_smem.wait()

    def pack(o, carry):
        send_r[o] = cache[:, idxs[0, o]]
        return carry

    lax.fori_loop(0, 32, pack, 0)

    relocate(0)
    own_block = pltpu.make_async_copy(send_r.at[0], recv_r.at[0], lsem.at[12])
    own_block.start()

    for load in loads[4:9]:
        load.wait()
    res = res_ref[...].astype(F32)
    nks[0:4] = nkv_ref[:, 0].astype(F32)
    nks[4:8] = nkv_ref[:, 0].astype(F32)
    nvs[0:4] = nkv_ref[:, 1].astype(F32)
    nvs[4:8] = nkv_ref[:, 1].astype(F32)
    for i in range(6):
        res_s[4 * i : 4 * i + 4] = res[:, 128 * i : 128 * i + 128]
    s8, b8 = iota((8, 128), 0), iota((8, 128), 1)
    low = jnp.where((s8 < 4) & (b8 == 4 * c + s8), 1.0, 0.0).astype(BF16)
    high = jnp.where((s8 >= 4) & (b8 == 4 * c + s8 - 4), 1.0, 0.0).astype(BF16)
    q24 = jnp.concatenate([dot(low, q_ref[2 * p]) + dot(high, q_ref[2 * p + 1]) for p in range(3)], axis=0)
    nk24 = jnp.concatenate([nks[...]] * 3, axis=0)
    nv24 = jnp.concatenate([nvs[...]] * 3, axis=0)
    own_score = jnp.sum(q24 * nk24, axis=1, keepdims=True) * scale
    eye24 = iota((24, 128), 0) == iota((24, 128), 1)
    own_score = jnp.sum(jnp.where(eye24, own_score, 0.0), axis=0, keepdims=True)

    g3 = split3(gates_ref[...])
    scr[0:2] = ids_ref[...].astype(F32)
    for i in range(3):
        scr[2 * i + 2 : 2 * i + 4] = g3[i]
    o128 = rlane >> 2
    group = ((x - (o128 >> 3)) & 3) * 8 + ((z - (o128 & 7)) & 7)
    relative = jnp.where(rsub == 4 * group + (rlane & 3), 1.0, 0.0).astype(BF16)
    routed = dot(scr[...].astype(BF16), relative)
    r0, r1 = routed[0:1].astype(I32), routed[1:2].astype(I32)
    w0 = routed[2:3] + routed[4:5] + routed[6:7]
    w1 = routed[3:4] + routed[5:6] + routed[7:8]
    goes = jnp.where((r0 == s8) | (r1 == s8), 1, 0)
    rank = jnp.zeros((8, 128), I32)
    for d in range(1, 4):
        rank = rank + jnp.where((b8 & 3) >= d, pltpu.roll(goes, d, 1), 0)
    slot = jnp.where(goes > 0, ((b8 >> 2) << 1) + rank, -1)
    slots[...] = slot
    gatev[...] = jnp.where(r0 == s8, w0, 0.0) + jnp.where(r1 == s8, w1, 0.0)
    row64 = iota((64, 128), 0)
    sel = jnp.concatenate([jnp.where(row64 == slot[j : j + 1], 1.0, 0.0) for j in range(8)], axis=0)
    picks = []
    for dx in range(4):
        block = jnp.concatenate([sel[64 * j + 16 * dx : 64 * j + 16 * dx + 16] for j in range(8)], axis=0)
        if dx:
            block = pltpu.roll(block, 128 - 32 * dx, 1)
        picks.append(block[:, 0:32].astype(BF16))
    far_rows = jnp.concatenate([sel[64 * j + 16 : 64 * j + 64] for j in range(8)], axis=0).T
    near_rows = jnp.concatenate([sel[64 * j : 64 * j + 16] for j in range(8)], axis=0).T
    sel_far[...] = far_rows[32:128].astype(BF16)
    sel_near[...] = near_rows[0:32].astype(BF16)
    gate_col = jnp.sum(
        jnp.where(row64 == slots[pl.ds(e, 1)], gatev[pl.ds(e, 1)], 0.0), axis=1, keepdims=True
    )

    def unpack(got):
        st = got[:, 24:32]
        qi = iota(st.shape, 1)
        m = jnp.sum(jnp.where(qi < 3, st, 0.0), axis=1, keepdims=True)
        l = jnp.sum(jnp.where((qi >= 3) & (qi < 6), st, 0.0), axis=1, keepdims=True)
        return jnp.where(l > 0, m, NEG), l

    def column(w):
        wide = jnp.broadcast_to(w, (w.shape[0], 24, 128))
        return jnp.sum(jnp.where(eye24[None], wide, 0.0), axis=2, keepdims=True)

    loop(1, 4, lambda dx: copy_a(dx).wait_recv())
    got = recv_a[...].astype(F32).reshape(32, 32, 128)
    m, l = unpack(got)
    m, l = m.reshape(4, 8, 1, 128), l.reshape(4, 8, 1, 128)
    top = jnp.max(m, axis=0)
    w = jnp.where(l > 0, jnp.exp(m - top[None]), 0.0)
    l = jnp.sum(w * l, axis=0)
    parts = split3(jnp.where(l > 0, top, 0.0)) + split3(l)
    qi = iota((8, 8, 128), 1)
    stat = jnp.zeros((8, 8, 128), F32)
    for n in range(6):
        stat = jnp.where(qi == n, parts[n], stat)
    values = column(w.reshape(32, 1, 128)) * got[:, 0:24]
    values = jnp.sum(values.reshape(4, 8, 24, 128), axis=0)
    send_b[...] = jnp.concatenate([values, stat], axis=1).astype(BF16)
    loop(1, 8, lambda dz: copy_b(dz).start())
    recv_b[0] = send_b[z]
    relocate(1)
    loop(1, 8, lambda dz: copy_b(dz).wait_recv())
    got = recv_b[...].astype(F32)
    m, l = unpack(got)
    top = jnp.maximum(jnp.max(m, axis=0), own_score)
    w = jnp.where(l > 0, jnp.exp(m - top[None]), 0.0)
    fresh = jnp.exp(own_score - top)
    inv_den = 1.0 / (jnp.sum(w * l, axis=0) + fresh)
    att = jnp.sum(column(w * inv_den[None]) * got[:, 0:24], axis=0)
    fcol = jnp.sum(jnp.where(eye24, fresh * inv_den, 0.0), axis=1, keepdims=True)
    att = att + fcol * nv24
    hidden = (res_s[...] + att).astype(BF16).astype(F32)
    gx[0, 0] = jnp.concatenate([hidden, jnp.zeros((8, 128), F32)], axis=0).astype(BF16)

    def copy_c(dz):
        return remote(gx.at[0, 0], gx.at[0, dz], sc.at[dz], rc.at[dz], ctx=ctx_at(0, dz))

    def copy_d(dx):
        return remote(gx.at[0], gx.at[dx], sd.at[dx], rd.at[dx], ctx=ctx_at(dx, 0))

    def copy_e(dx, o):
        t = exp_at(lax.div(o, 2), lax.rem(o, 2))
        rows = pl.ds(16 * dx, 16)
        return remote(send_e.at[t, rows], recv_e.at[e, rows], se.at[8 * dx + o], re.at[8 * dx + o], exp=t)

    def dispatch(dx):
        flat = gx[dx].astype(F32).reshape(4, 2, 32, 128)
        parts = []
        for p in range(3):
            one, two = flat[:, 0, 8 * p : 8 * p + 8], flat[:, 1, 8 * p : 8 * p + 8]
            parts.append(jnp.where(sub4 < 4, one, pltpu.roll(two, 4, 1)).reshape(32, 128).astype(BF16))
            parts.append(jnp.where(sub4 < 4, pltpu.roll(one, 4, 1), two).reshape(32, 128).astype(BF16))
        rows = dot(picks[dx], jnp.concatenate(parts, axis=1)).astype(BF16)
        for j in range(8):
            send_e[j, 16 * dx : 16 * dx + 16] = rows[16 * j : 16 * j + 16]
        loop(1, 8, lambda o: copy_e(dx, o).start())

    sub4 = iota((4, 8, 128), 1)
    loop(1, 8, lambda dz: copy_c(dz).start())
    relocate(2)
    loop(1, 8, lambda dz: copy_c(dz).wait_recv())
    loop(1, 4, lambda dx: copy_d(dx).start())
    dispatch(0)
    relocate(3)
    for dx in (1, 3, 2):
        copy_d(dx).wait_recv()
        dispatch(dx)
    relocate(4)
    recv_e[e] = send_e[e]
    loads[9].wait()

    def first_half(o, carry):
        gate, upper, square = carry
        src = lax.rem(y + 4 - lax.div(o, 2), 4) * 2 + lax.rem(k + lax.rem(o, 2), 2)
        rows = recv_e[src].astype(F32)
        square = square + jnp.sum(rows * rows, axis=1, keepdims=True)
        gain = jnp.concatenate([gain_ref[pl.ds(6 * src + i, 1)] for i in range(6)], axis=1)
        scaled = (rows * gain).astype(BF16)
        start = pl.multiple_of(src * 768, 768)
        gate = gate + dot(scaled, win[0, pl.ds(start, 768)])
        upper = upper + dot(scaled, win[1, pl.ds(start, 768)])
        return gate, upper, square

    def arrived(o, carry):
        for dx in (0, 1, 3, 2):
            copy_e(dx, o).wait_recv()
        return first_half(o, carry)

    zero = jnp.zeros((64, 256), F32)
    carry = first_half(0, (zero, zero, jnp.zeros((64, 1), F32)))
    gate, upper, square = lax.fori_loop(1, 8, arrived, carry)
    inverse = lax.rsqrt(square * (1.0 / 6144) + EPS)
    gate = gate * inverse
    act = (gate / (1.0 + jnp.exp(-gate)) * (upper * inverse)).astype(BF16)
    loads[10].wait()

    def copy_f(o):
        t = exp_at(lax.div(o, 2), lax.rem(o, 2))
        return remote(send_f.at[t], recv_f.at[e], sf.at[o], rf.at[o], exp=t)

    def copy_n(o):
        t = exp_at(lax.div(o, 2), lax.rem(o, 2))
        return remote(send_n.at[t], recv_n.at[e], sn.at[o], rn.at[o], exp=t)

    def second_half(t):
        start = pl.multiple_of(t * 768, 768)
        return (dot(act, wout[:, pl.ds(start, 768)]) * gate_col).astype(BF16)

    def produce(n):
        o = 8 - n
        t = exp_at(lax.div(o, 2), lax.rem(o, 2))
        rows = second_half(t)
        send_f[t] = rows[16:64]
        send_n[t] = rows[0:16]
        copy_f(o).start()

    loop(1, 8, produce)
    loop(1, 8, lambda o: copy_n(o).start())
    relocate(5)
    rows = second_half(e)
    recv_f[e] = rows[16:64]
    recv_n[e] = rows[0:16]
    loop(1, 8, lambda o: copy_f(o).wait_recv())
    mixed = dot(sel_far[...], recv_f[...].reshape(384, 768))
    for dx in range(1, 4):
        send_g[dx] = mixed[32 * dx - 32 : 32 * dx].astype(BF16)

    def copy_g(dx):
        return remote(send_g.at[dx], recv_g.at[dx], sg.at[dx], rg.at[dx], ctx=ctx_at(4 - dx, 0))

    def copy_h(dz):
        return remote(send_h.at[dz], recv_h.at[dz], sh.at[dz], rh.at[dz], ctx=ctx_at(0, 8 - dz))

    loop(1, 4, lambda dx: copy_g(dx).start())
    loop(1, 8, lambda o: copy_n(o).wait_recv())
    mixed = dot(sel_near[...], recv_n[...].reshape(128, 768))
    relocate(6)
    loop(1, 4, lambda dx: copy_g(dx).wait_recv())
    summed = mixed + recv_g[1].astype(F32) + recv_g[2].astype(F32) + recv_g[3].astype(F32)
    cols = [summed[:, 128 * i : 128 * i + 128].reshape(4, 8, 128) for i in range(6)]
    evens, odds = [], []
    for p in range(3):
        one, two = cols[2 * p], cols[2 * p + 1]
        evens.append(jnp.where(sub4 < 4, one, pltpu.roll(two, 4, 1)))
        odds.append(jnp.where(sub4 < 4, pltpu.roll(one, 4, 1), two))
    pad = [jnp.zeros((4, 8, 128), F32)]
    evens, odds = jnp.concatenate(evens + pad, axis=1), jnp.concatenate(odds + pad, axis=1)
    for n in range(4):
        send_h[2 * n] = evens[n].astype(BF16)
        send_h[2 * n + 1] = odds[n].astype(BF16)
    loop(1, 8, lambda dz: copy_h(dz).start())
    relocate(7)

    loop(1, 8, lambda dz: copy_h(dz).wait_recv())
    total = hidden + evens[0, 0:24]
    for dz in range(1, 8):
        total = total + recv_h[dz].astype(F32)[0:24]
    att_s[...] = total
    for i in range(6):
        lay_ref[:, 128 * i : 128 * i + 128] = att_s[4 * i : 4 * i + 4].astype(BF16)

    own_block.wait()
    loop(1, 32, lambda o: copy_r(o, lax.div(o, 8), lax.rem(o, 8)).wait_recv())
    loop(1, 4, lambda dx: copy_a(dx).wait_send())
    loop(1, 8, lambda dz: copy_b(dz).wait_send())
    loop(1, 8, lambda dz: copy_c(dz).wait_send())
    loop(1, 4, lambda dx: copy_d(dx).wait_send())
    for dx in range(4):
        loop(1, 8, lambda o, dx=dx: copy_e(dx, o).wait_send())
    loop(1, 8, lambda o: copy_f(o).wait_send())
    loop(1, 8, lambda o: copy_n(o).wait_send())
    loop(1, 4, lambda dx: copy_g(dx).wait_send())
    loop(1, 8, lambda dz: copy_h(dz).wait_send())
    loop(1, 32, lambda o: copy_r(o, lax.div(o, 8), lax.rem(o, 8)).wait_send())


def place_blocks(idxs, layer_ref, blocks_hbm, lay_ref, fin_hbm, held, came, went):
    def load(s):
        return pltpu.make_async_copy(blocks_hbm.at[idxs[1, s]], held.at[s], came.at[s])

    def store(s):
        return pltpu.make_async_copy(held.at[s], fin_hbm.at[:, s], went.at[s])

    def start(s, carry):
        @pl.when(idxs[2, s] > 0)
        def _():
            load(s).start()

        return carry

    def clear(s, carry):
        @pl.when(idxs[2, s] == 0)
        def _():
            held[s] = jnp.zeros((2, 128, 128), BF16)
            store(s).start()

        return carry

    def forward(s, carry):
        @pl.when(idxs[2, s] > 0)
        def _():
            load(s).wait()
            store(s).start()

        return carry

    def finish(s, carry):
        store(s).wait()
        return carry

    lax.fori_loop(0, 16, start, 0)
    lay_ref[...] = layer_ref[...]
    lax.fori_loop(0, 16, clear, 0)
    lax.fori_loop(0, 16, forward, 0)
    lax.fori_loop(0, 16, finish, 0)


def per_device(
    queries, new_kv, kv_cache, residual, kept_blocks, block_moves, expert_ids, gate_weights, norm_gain, expert_in,
    expert_out,
):
    vmem = pl.BlockSpec(memory_space=pltpu.VMEM)
    hbm = pl.BlockSpec(memory_space=pl.ANY)
    dma = pltpu.SemaphoreType.DMA
    layer, blocks, index = pl.pallas_call(
        kernel,
        out_shape=(
            jax.ShapeDtypeStruct((4, 768), BF16),
            jax.ShapeDtypeStruct((32, 2, 128, 128), BF16),
            jax.ShapeDtypeStruct((8, 128), I32),
        ),
        in_specs=[hbm] * 11,
        out_specs=(vmem, hbm, vmem),
        scratch_shapes=[
            pltpu.VMEM((1, 512), I32),
            pltpu.VMEM((2, 4, 128), I32),
            pltpu.VMEM((2, 16, 128, 128), BF16),
            pltpu.VMEM((6, 128, 128), BF16),
            pltpu.VMEM((4, 2, 128), BF16),
            pltpu.VMEM((4, 768), BF16),
            pltpu.VMEM((2, 128), I32),
            pltpu.VMEM((2, 128), F32),
            pltpu.VMEM((48, 128), F32),
            pltpu.VMEM((2, 6144, 256), BF16),
            pltpu.VMEM((256, 6144), BF16),
            pltpu.SMEM((8, 128), I32),
            pltpu.VMEM((4, 8, 32, 128), BF16),
            pltpu.VMEM((4, 8, 32, 128), BF16),
            pltpu.VMEM((8, 32, 128), BF16),
            pltpu.VMEM((8, 32, 128), BF16),
            pltpu.VMEM((4, 8, 32, 128), BF16),
            pltpu.VMEM((8, 64, 768), BF16),
            pltpu.VMEM((8, 64, 768), BF16),
            pltpu.VMEM((8, 48, 768), BF16),
            pltpu.VMEM((8, 48, 768), BF16),
            pltpu.VMEM((8, 16, 768), BF16),
            pltpu.VMEM((8, 16, 768), BF16),
            pltpu.VMEM((4, 32, 768), BF16),
            pltpu.VMEM((4, 32, 768), BF16),
            pltpu.VMEM((8, 32, 128), BF16),
            pltpu.VMEM((8, 32, 128), BF16),
            pltpu.VMEM((32, 2, 128, 128), BF16),
            pltpu.VMEM((8, 128), F32),
            pltpu.VMEM((8, 128), F32),
            pltpu.VMEM((8, 128), F32),
            pltpu.VMEM((8, 128), I32),
            pltpu.VMEM((8, 128), F32),
            pltpu.VMEM((96, 384), BF16),
            pltpu.VMEM((32, 128), BF16),
            pltpu.VMEM((24, 128), F32),
            pltpu.VMEM((24, 128), F32),
            dma((13,)),
            dma((4,)), dma((4,)),
            dma((8,)), dma((8,)),
            dma((8,)), dma((8,)),
            dma((4,)), dma((4,)),
            dma((32,)), dma((32,)),
            dma((8,)), dma((8,)),
            dma((8,)), dma((8,)),
            dma((4,)), dma((4,)),
            dma((8,)), dma((8,)),
            dma((32,)), dma((32,)),
        ],
        compiler_params=pltpu.CompilerParams(
            collective_id=0, has_side_effects=True, vmem_limit_bytes=60 * 1024 * 1024
        ),
        name="layer",
    )(
        block_moves.reshape(1, 512),
        jnp.transpose(kept_blocks[:, 0], (0, 2, 1)),
        kv_cache.reshape(2, 16, 128, 128),
        jnp.transpose(queries[0], (1, 0, 2)),
        new_kv.reshape(4, 2, 128),
        residual.reshape(4, 768),
        expert_ids[0].T,
        gate_weights[0].T,
        norm_gain.reshape(48, 128),
        expert_in.reshape(2, 6144, 256),
        expert_out.reshape(256, 6144),
    )
    layer, final = pl.pallas_call(
        place_blocks,
        out_shape=(
            jax.ShapeDtypeStruct((4, 768), BF16),
            jax.ShapeDtypeStruct((2, 16, 128, 128), BF16),
        ),
        in_specs=[pl.BlockSpec(memory_space=pltpu.SMEM), vmem, hbm],
        out_specs=(vmem, hbm),
        scratch_shapes=[pltpu.VMEM((16, 2, 128, 128), BF16), dma((16,)), dma((16,))],
        compiler_params=pltpu.CompilerParams(vmem_limit_bytes=60 * 1024 * 1024),
        name="place_blocks",
    )(index, layer, blocks)
    return layer.reshape(1, 4, 768), final.reshape(2, 1, 16, 128, 128)


def solution(mesh):
    in_specs = (
        P(None, None, "exp", None),
        P(None, "ctx", None, "exp", None),
        P(None, "exp", "ctx", None, None),
        P(None, "ctx", "exp"),
        P(None, "exp", None, None),
        P(None, "exp", None),
        P(),
        P(),
        P(),
        P("exp", None, None, "ctx"),
        P("exp", "ctx", None),
    )
    out_specs = (P(None, "ctx", "exp"), P(None, "exp", "ctx", None, None))
    return jax.shard_map(
        per_device, mesh=mesh, in_specs=in_specs, out_specs=out_specs, check_vma=False
    )
```
